128 devices in a mesh: dp: 16 (over z, y), grp: 8 (over x, core).
Axes of the slice: x: 4, y: 4, z: 4, core: 2. Of those that a mesh axis runs over, the one named last changes fastest.
Arguments:
- frames: bfloat16 [384, 256, 1024], P(('dp', 'grp')), may hold values from -6 to 6
- episode_len: int32 [48], replicated, may hold values from 1 to 64, 384 in all
- norm_spatial: float32 [1024], replicated, may hold values from 0.25 to 1.75
- w_sqkv: bfloat16 [1024, 3072], replicated
- w_so: bfloat16 [1024, 1024], replicated, may hold values from -0.1875 to 0.1875
- norm_temporal: float32 [1024], replicated, may hold values from 0.25 to 1.75
- w_tqkv: bfloat16 [1024, 3072], P(('dp', 'grp'))
- w_to: bfloat16 [1024, 1024], P(('dp', 'grp')), may hold values from -0.1875 to 0.1875
Outputs:
- block_out: bfloat16 [384, 256, 1024], P(('dp', 'grp'))
The draws below stay inside these ranges and needn't reach their ends.
Inputs may be any that keep to these rules, and one draw needn't show every extreme that they name: episode_len lists consecutive episodes that together cover all 384 frames; the longest has exactly 64 frames.
All inputs are finite; a program needn't handle non-finite values.
Results may differ from the reference program's by a relative error of at most 0.029.
The reference program's roundings to bfloat16 on the way count: a program that leaves them out, or rounds other values in their place, can miss the bound.
Values may be sent and summed in bfloat16 or wider, within the bound.
No kernel may reach another device: no remote copies, remote signals or barrier semaphores. Data moves between devices by JAX's collectives and lax.ppermute only.
A program may use at most 128 MiB of HBM per device.

```python
import math
import jax
import jax.numpy as jnp
import numpy as np
from jax import lax

D = 1024
HEADS = 16
HEAD_DIM = 64
P_SIZE = 256
FRAMES = 384
MAX_EP = 64
EPISODES = 48


def draw_w_sqkv(key, part):
    key = jax.random.fold_in(key, 11)
    values = jax.random.normal(key, (D, 3 * D), jnp.float32) * D ** (-0.5)
    return values.astype(jnp.bfloat16)


def draw_w_tqkv(key, part):
    key = jax.random.fold_in(key, 23)
    values = jax.random.normal(key, (D, 3 * D), jnp.float32) * D ** (-0.5)
    return values.astype(jnp.bfloat16)


def shard_levels(own_key, shape, shards, least, high):
    def one(dim, parts):
        steps = jax.random.uniform(jax.random.fold_in(jax.random.fold_in(own_key, 6), dim), (parts,), jnp.float32, least / len(shards), high / len(shards))
        return jnp.repeat(jnp.exp(steps), shape[dim] // parts).reshape((-1,) + (1,) * (len(shape) - dim - 1))

    factor_of = one(*shards[0])
    for cut in shards[1:]:
        factor_of = factor_of * one(*cut)
    return factor_of


def profile(count, total, reach, lean):
    loads = [(1 << 20) // math.isqrt(standing ** lean) + 1 for standing in range(2, count + 1)]
    rest, holding = total - reach - (count - 1), [1] * (count - 1)
    while rest > 0:
        free = [i for i in range(count - 1) if holding[i] < reach]
        mass, budget = sum([loads[i] for i in free]), rest
        for i in free:
            extra = min(reach - holding[i], max(1, budget * loads[i] // mass), rest)
            holding[i] = holding[i] + extra
            rest = rest - extra
    return np.array([reach] + holding)


def uneven(own_key, number_of, total, limit, skew):
    if number_of == 2:
        one = jax.random.randint(own_key, (), max(1, total - limit), min(limit, total - 1) + 1)
        return jnp.stack([one, total - one])
    sizes = jnp.asarray(profile(number_of, total, limit, skew), jnp.int32)
    pairs = (number_of - 1) // 2
    source_of, taker = sizes[1:1 + 2 * pairs:2], sizes[2:2 + 2 * pairs:2]
    slack = jnp.minimum(source_of - 1, limit - taker)
    shifted = jax.random.randint(jax.random.fold_in(own_key, 1), (pairs,), 0, 1 << 20) % (slack + 1)
    sizes = sizes.at[1:1 + 2 * pairs:2].set(source_of - shifted).at[2:2 + 2 * pairs:2].set(taker + shifted)
    return sizes[jax.random.permutation(jax.random.fold_in(own_key, 2), number_of)]


def scatter_about(stream_key, dims, spread, limit, cuts=(), kind=jnp.bfloat16):
    level = shard_levels(stream_key, dims, cuts, -0.22, 0.18) if cuts else 1.0
    drawn = jax.random.normal(stream_key, dims, jnp.float32) * spread * level
    return jnp.minimum(jnp.maximum(drawn, -limit), limit).astype(kind)


def setup_inputs(seed: int = 0) -> dict:
    arg_keys = jax.random.split(jax.random.key(seed), 9)
    frames = scatter_about(arg_keys[0], (FRAMES, P_SIZE, D), 1.0, 6.0, ((0, 128),))
    episode_len = uneven(arg_keys[1], EPISODES, FRAMES, MAX_EP, 2).astype(jnp.int32)
    norm_spatial = jnp.clip(1.0 + 0.15 * jax.random.normal(arg_keys[2], (D,), jnp.float32), 0.25, 1.75)
    w_sqkv = draw_w_sqkv(jax.random.fold_in(arg_keys[8], 71), 0)
    w_so = scatter_about(arg_keys[4], (D, D), D ** -0.5, 0.1875)
    norm_temporal = jnp.clip(1.0 + 0.15 * jax.random.normal(arg_keys[5], (D,), jnp.float32), 0.25, 1.75)
    w_tqkv = draw_w_tqkv(jax.random.fold_in(arg_keys[8], 71), 0)
    w_to = scatter_about(arg_keys[7], (D, D), D ** -0.5, 0.1875, ((0, 128),))
    return {"frames": frames, "episode_len": episode_len, "norm_spatial": norm_spatial, "w_sqkv": w_sqkv, "w_so": w_so, "norm_temporal": norm_temporal, "w_tqkv": w_tqkv, "w_to": w_to}


def normed(values, gain):
    wide = values.astype(jnp.float32)
    scale = lax.rsqrt(lax.optimization_barrier(jnp.mean(wide * wide, axis=-1, keepdims=True)) + 1e-06)
    return (wide * scale * gain).astype(jnp.bfloat16)

def softmax_rows(scores):
    top = lax.optimization_barrier(jnp.max(scores, axis=-1, keepdims=True))
    weights = jnp.exp(scores - top)
    return (weights / lax.optimization_barrier(jnp.sum(weights, axis=-1, keepdims=True))).astype(jnp.bfloat16)

def reference(frames, episode_len, norm_spatial, w_sqkv, w_so, norm_temporal, w_tqkv, w_to):
    scale = HEAD_DIM ** (-0.5)

    def spatial(frame):
        hidden = normed(frame, norm_spatial)
        qkv = jnp.dot(hidden, w_sqkv, preferred_element_type=jnp.float32).astype(jnp.bfloat16)
        qkv = qkv.reshape(P_SIZE, 3, HEADS, HEAD_DIM).astype(jnp.float32)
        scores = jnp.einsum('phd,qhd->hpq', qkv[:, 0], qkv[:, 1]) * scale
        probs = softmax_rows(scores).astype(jnp.float32)
        heads = jnp.einsum('hpq,qhd->phd', probs, qkv[:, 2]).astype(jnp.bfloat16).reshape(P_SIZE, D)
        update = jnp.dot(heads, w_so, preferred_element_type=jnp.float32)
        return (frame.astype(jnp.float32) + update).astype(jnp.bfloat16)
    mixed = lax.map(spatial, frames)
    ends = jnp.cumsum(episode_len)
    position = jnp.arange(FRAMES, dtype=jnp.int32)
    episode = lax.optimization_barrier(jnp.sum((position[:, None] >= ends[None, :]).astype(jnp.int32), axis=1))
    allowed = (position[None, :] <= position[:, None]) & (episode[None, :] == episode[:, None])

    def temporal(column):
        hidden = normed(column, norm_temporal)
        qkv = jnp.dot(hidden, w_tqkv, preferred_element_type=jnp.float32).astype(jnp.bfloat16)
        qkv = qkv.reshape(FRAMES, 3, HEADS, HEAD_DIM).astype(jnp.float32)
        scores = jnp.einsum('fhd,ghd->hfg', qkv[:, 0], qkv[:, 1]) * scale
        scores = jnp.where(allowed[None], scores, -1e+30)
        probs = softmax_rows(scores).astype(jnp.float32)
        heads = jnp.einsum('hfg,ghd->fhd', probs, qkv[:, 2]).astype(jnp.bfloat16).reshape(FRAMES, D)
        return jnp.dot(heads, w_to, preferred_element_type=jnp.float32).astype(jnp.bfloat16)
    updates = lax.map(temporal, jnp.transpose(mixed, (1, 0, 2)))
    updates = jnp.transpose(updates, (1, 0, 2))
    return (mixed.astype(jnp.float32) + updates.astype(jnp.float32)).astype(jnp.bfloat16)
```

```python
import functools

import jax
import jax.numpy as jnp
from jax import lax
from jax.experimental import pallas as pl
from jax.experimental.pallas import tpu as pltpu
from jax.sharding import PartitionSpec as P

HEADS = 16
LANES = 128
CHUNK = 256
LOG2E = 1.4426950408889634
F32 = jnp.float32
BF16 = jnp.bfloat16


def normed(wide, gain):
    scale = lax.rsqrt(jnp.mean(wide * wide, axis=-1, keepdims=True) + 1e-06)
    return wide * scale * gain


def head_pair(q2, k2, v2, scale, cap=None):
    lane = lax.broadcasted_iota(jnp.int32, q2.shape, 1)
    zero = jnp.zeros_like(q2)
    outs = []
    for side in range(2):
        mine = lane < 64 if side == 0 else lane >= 64
        q = jnp.where(mine, q2, zero)
        scores = lax.dot_general(q, k2, (((1,), (1,)), ((), ())), preferred_element_type=F32)
        if cap is not None:
            scores = jnp.minimum(scores, cap)
        top = jnp.max(scores, axis=-1, keepdims=True)
        weights = jnp.exp2((scores - top) * (scale * LOG2E))
        total = jnp.sum(weights, axis=-1, keepdims=True)
        out = jnp.dot(weights.astype(BF16), v2, preferred_element_type=F32)
        outs.append(out * (1.0 / total))
    return jnp.where(lane < 64, outs[0], outs[1]).astype(BF16)


def spatial_kernel(
    tokens,
    frames_ref,
    gain_s_ref,
    gain_t_ref,
    w_qkv_hbm,
    w_o_hbm,
    mixed_ref,
    send_ref,
    w_qkv,
    w_o,
    hidden,
    qkv,
    heads,
    stage,
    qkv_sem,
    o_sem,
):
    rows, width = frames_ref.shape
    count = rows // tokens
    parts = 3 * width // CHUNK
    scale = (width // HEADS) ** (-0.5)
    groups = width // LANES
    owners = tokens // 2
    block = count * 2 * groups

    def fetch(c):
        return pltpu.make_async_copy(
            w_qkv_hbm.at[:, pl.ds(pl.multiple_of(c * CHUNK, CHUNK), CHUNK)], w_qkv.at[c], qkv_sem.at[c]
        )

    fetch_o = pltpu.make_async_copy(w_o_hbm, w_o, o_sem)
    for c in range(parts):
        fetch(c).start()
    fetch_o.start()

    @pl.loop(0, count)
    def _(f):
        at = pl.ds(pl.multiple_of(f * tokens, tokens), tokens)
        hidden[at, :] = normed(frames_ref[at, :].astype(F32), gain_s_ref[...]).astype(BF16)

    @pl.loop(0, parts)
    def _(c):
        fetch(c).wait()
        qkv[c] = jnp.dot(hidden[...], w_qkv[c], preferred_element_type=F32).astype(BF16)

    fetch_o.wait()
    third = parts // 3
    per = CHUNK // LANES

    @pl.loop(0, count)
    def _(f):
        at = pl.ds(pl.multiple_of(f * tokens, tokens), tokens)
        for pair in range(HEADS // 2):
            c, cols = pair // per, pl.ds((pair % per) * LANES, LANES)
            heads[:, pair * LANES : (pair + 1) * LANES] = head_pair(
                qkv[c, at, cols], qkv[third + c, at, cols], qkv[2 * third + c, at, cols], scale
            )
        update = jnp.dot(heads[...], w_o[...], preferred_element_type=F32)
        mixed = (frames_ref[at, :].astype(F32) + update).astype(BF16)
        mixed_ref[at, :] = mixed
        inner = normed(mixed.astype(F32), gain_t_ref[...])
        for i in range(2):
            for j in range(groups):
                stage[pl.ds(f * 2 * groups + i * groups + j, owners, stride=block), :] = inner[
                    i * owners : (i + 1) * owners, j * LANES : (j + 1) * LANES
                ]

    send_ref[...] = stage[...].astype(BF16)


def spatial(frames, gain_s, gain_t, w_qkv, w_o):
    count, tokens, width = frames.shape
    rows = count * tokens
    parts = 3 * width // CHUNK
    vmem = pl.BlockSpec(memory_space=pltpu.VMEM)
    hbm = pl.BlockSpec(memory_space=pl.ANY)
    return pl.pallas_call(
        functools.partial(spatial_kernel, tokens),
        out_shape=(
            jax.ShapeDtypeStruct((rows, width), BF16),
            jax.ShapeDtypeStruct((rows * width // LANES, LANES), BF16),
        ),
        in_specs=[vmem, vmem, vmem, hbm, hbm],
        out_specs=(vmem, vmem),
        scratch_shapes=[
            pltpu.VMEM((parts, width, CHUNK), BF16),
            pltpu.VMEM((width, width), BF16),
            pltpu.VMEM((rows, width), BF16),
            pltpu.VMEM((parts, rows, CHUNK), BF16),
            pltpu.VMEM((tokens, width), BF16),
            pltpu.VMEM((rows * width // LANES, LANES), F32),
            pltpu.SemaphoreType.DMA((parts,)),
            pltpu.SemaphoreType.DMA,
        ],
        compiler_params=pltpu.CompilerParams(vmem_limit_bytes=44 * 2**20),
        cost_estimate=pl.CostEstimate(flops=16 * 10**9, bytes_accessed=14 * 2**20, transcendentals=0),
        name="spatial",
    )(frames.reshape(rows, width), gain_s.reshape(1, width), gain_t.reshape(1, width), w_qkv, w_o)


def temporal_kernel(
    local_pos,
    len_ref,
    recv_ref,
    w_qkv_hbm,
    w_o_hbm,
    send_ref,
    w_qkv,
    w_o,
    hidden,
    qkv,
    heads,
    stage,
    cap,
    qkv_sem,
    o_sem,
):
    total = hidden.shape[0] // local_pos
    width = hidden.shape[1]
    parts = 3 * width // CHUNK
    scale = (width // HEADS) ** (-0.5)
    groups = width // LANES
    block = local_pos * groups
    span = cap.shape[1]

    def fetch(c):
        return pltpu.make_async_copy(
            w_qkv_hbm.at[:, pl.ds(pl.multiple_of(c * CHUNK, CHUNK), CHUNK)], w_qkv.at[c], qkv_sem.at[c]
        )

    fetch_o = pltpu.make_async_copy(w_o_hbm, w_o, o_sem)
    for c in range(parts):
        fetch(c).start()
    fetch_o.start()

    position = lax.broadcasted_iota(jnp.int32, (total, LANES), 0)

    def first(e, carry):
        end, begin = carry
        end = end + len_ref[e]
        return end, jnp.where(position >= end, end, begin)

    _, begin = lax.fori_loop(0, len_ref.shape[0], first, (jnp.int32(0), jnp.zeros((total, LANES), jnp.int32)))
    lane = lax.broadcasted_iota(jnp.int32, (span, LANES), 1)
    for b in range(total // span):
        rows = slice(b * span, (b + 1) * span)
        for side in range(2):
            other = lane + (b - 1 + side) * span
            fine = (other <= position[rows]) & (other >= begin[rows])
            cap[b, :, side * span : (side + 1) * span] = jnp.where(fine, jnp.inf, -1e30)

    stage[...] = recv_ref[...].astype(F32)
    for i in range(local_pos):
        for j in range(groups):
            hidden[i * total : (i + 1) * total, j * LANES : (j + 1) * LANES] = stage[
                pl.ds(i * groups + j, total, stride=block), :
            ].astype(BF16)

    @pl.loop(0, parts)
    def _(c):
        fetch(c).wait()
        qkv[c] = jnp.dot(hidden[...], w_qkv[c], preferred_element_type=F32).astype(BF16)

    fetch_o.wait()
    third = parts // 3
    per = CHUNK // LANES

    for i in range(local_pos):
        for b in range(total // span):
            at = pl.ds(i * total + b * span, span)
            low = max(b - 1, 0)
            seen = pl.ds(i * total + low * span, (b + 1 - low) * span)
            limit = cap[b] if b else cap[b, :, span:]
            for pair in range(HEADS // 2):
                c, cols = pair // per, pl.ds((pair % per) * LANES, LANES)
                heads[b * span : (b + 1) * span, pair * LANES : (pair + 1) * LANES] = head_pair(
                    qkv[c, at, cols], qkv[third + c, seen, cols], qkv[2 * third + c, seen, cols], scale, limit
                )
        update = jnp.dot(heads[...], w_o[...], preferred_element_type=F32)
        for j in range(groups):
            stage[pl.ds(i * groups + j, total, stride=block), :] = update[:, j * LANES : (j + 1) * LANES]

    send_ref[...] = stage[...].astype(BF16)


def temporal(episode_len, recv, w_qkv, w_o, total, local_pos):
    width = w_o.shape[0]
    rows = total * local_pos
    parts = 3 * width // CHUNK
    span = LANES
    vmem = pl.BlockSpec(memory_space=pltpu.VMEM)
    hbm = pl.BlockSpec(memory_space=pl.ANY)
    return pl.pallas_call(
        functools.partial(temporal_kernel, local_pos),
        out_shape=jax.ShapeDtypeStruct(recv.shape, BF16),
        in_specs=[pl.BlockSpec(memory_space=pltpu.SMEM), vmem, hbm, hbm],
        out_specs=vmem,
        scratch_shapes=[
            pltpu.VMEM((parts, width, CHUNK), BF16),
            pltpu.VMEM((width, width), BF16),
            pltpu.VMEM((rows, width), BF16),
            pltpu.VMEM((parts, rows, CHUNK), BF16),
            pltpu.VMEM((total, width), BF16),
            pltpu.VMEM((rows * width // LANES, LANES), F32),
            pltpu.VMEM((total // span, span, 2 * span), F32),
            pltpu.SemaphoreType.DMA((parts,)),
            pltpu.SemaphoreType.DMA,
        ],
        compiler_params=pltpu.CompilerParams(vmem_limit_bytes=44 * 2**20),
        cost_estimate=pl.CostEstimate(flops=16 * 10**9, bytes_accessed=14 * 2**20, transcendentals=0),
        name="temporal",
    )(episode_len, recv, w_qkv, w_o)


def finish_kernel(tokens, mixed_ref, recv_ref, out_ref, stage):
    rows, width = mixed_ref.shape
    count = rows // tokens
    groups = width // LANES
    owners = tokens // 2
    block = count * 2 * groups
    stage[...] = recv_ref[...].astype(F32)
    for f in range(count):
        for i in range(2):
            for j in range(groups):
                at = (pl.ds(f * tokens + i * owners, owners), pl.ds(j * LANES, LANES))
                back = stage[pl.ds(f * 2 * groups + i * groups + j, owners, stride=block), :]
                out_ref[at] = (mixed_ref[at].astype(F32) + back).astype(BF16)


def finish(mixed, recv, tokens):
    vmem = pl.BlockSpec(memory_space=pltpu.VMEM)
    return pl.pallas_call(
        functools.partial(finish_kernel, tokens),
        out_shape=jax.ShapeDtypeStruct(mixed.shape, BF16),
        in_specs=[vmem, vmem],
        out_specs=vmem,
        scratch_shapes=[pltpu.VMEM(recv.shape, F32)],
        compiler_params=pltpu.CompilerParams(vmem_limit_bytes=32 * 2**20),
        name="finish",
    )(mixed, recv)


def local(frames, episode_len, norm_spatial, w_sqkv, w_so, norm_temporal, w_tqkv, w_to):
    axes = ("dp", "grp")
    count, tokens, width = frames.shape
    shards = lax.axis_size(axes)
    full_tqkv = lax.all_gather(w_tqkv, axes, axis=0, tiled=True)
    full_to = lax.all_gather(w_to, axes, axis=0, tiled=True)
    mixed, send = spatial(frames, norm_spatial, norm_temporal, w_sqkv, w_so)
    block = (shards, -1, LANES)
    recv = lax.all_to_all(send.reshape(block), axes, split_axis=0, concat_axis=0, tiled=True)
    back = temporal(
        episode_len, recv.reshape(-1, LANES), full_tqkv, full_to, count * shards, tokens // shards
    )
    returned = lax.all_to_all(back.reshape(block), axes, split_axis=0, concat_axis=0, tiled=True)
    return finish(mixed, returned.reshape(-1, LANES), tokens).reshape(frames.shape)


def solution(mesh):
    placed = (
        P(("dp", "grp"), None, None),
        P(),
        P(),
        P(),
        P(),
        P(),
        P(("dp", "grp"), None),
        P(("dp", "grp"), None),
    )
    return jax.shard_map(
        local, mesh=mesh, in_specs=placed, out_specs=P(("dp", "grp"), None, None), check_vma=False
    )
```

```python
import functools

import jax
import jax.numpy as jnp
from jax import lax
from jax.experimental import pallas as pl
from jax.experimental.pallas import tpu as pltpu
from jax.sharding import PartitionSpec as P

HEADS = 16
LANES = 128
CHUNK = 256
LOG2E = 1.4426950408889634
F32 = jnp.float32
BF16 = jnp.bfloat16


def normed(wide, gain):
    scale = lax.rsqrt(jnp.mean(wide * wide, axis=-1, keepdims=True) + 1e-06)
    return wide * scale * gain


def head_pair(q2, k2, v2, scale, cap=None):
    lane = lax.broadcasted_iota(jnp.int32, q2.shape, 1)
    zero = jnp.zeros_like(q2)
    outs = []
    for side in range(2):
        mine = lane < 64 if side == 0 else lane >= 64
        q = jnp.where(mine, q2, zero)
        scores = lax.dot_general(q, k2, (((1,), (1,)), ((), ())), preferred_element_type=F32)
        if cap is not None:
            scores = jnp.minimum(scores, cap)
        top = jnp.max(scores, axis=-1, keepdims=True)
        weights = jnp.exp2((scores - top) * (scale * LOG2E))
        total = jnp.sum(weights, axis=-1, keepdims=True)
        out = jnp.dot(weights.astype(BF16), v2, preferred_element_type=F32)
        outs.append(out * (1.0 / total))
    return jnp.where(lane < 64, outs[0], outs[1]).astype(BF16)


def spatial_kernel(
    tokens,
    frames_hbm,
    gain_s_ref,
    gain_t_ref,
    w_qkv_hbm,
    w_o_hbm,
    mixed_ref,
    send_ref,
    frames_ref,
    w_qkv,
    w_o,
    hidden,
    qkv,
    heads,
    stage,
    frame_sem,
    qkv_sem,
    o_sem,
):
    rows, width = frames_ref.shape
    count = rows // tokens
    parts = 3 * width // CHUNK
    scale = (width // HEADS) ** (-0.5)
    groups = width // LANES
    owners = tokens // 2
    block = count * 2 * groups

    def fetch(c):
        return pltpu.make_async_copy(
            w_qkv_hbm.at[:, pl.ds(pl.multiple_of(c * CHUNK, CHUNK), CHUNK)], w_qkv.at[c], qkv_sem.at[c]
        )

    fetch_o = pltpu.make_async_copy(w_o_hbm, w_o, o_sem)

    def fetch_frame(f):
        at = pl.ds(pl.multiple_of(f * tokens, tokens), tokens)
        return pltpu.make_async_copy(frames_hbm.at[at, :], frames_ref.at[at, :], frame_sem.at[f])

    for f in range(count):
        fetch_frame(f).start()
    for c in range(parts):
        fetch(c).start()
    fetch_o.start()

    @pl.loop(0, count)
    def _(f):
        at = pl.ds(pl.multiple_of(f * tokens, tokens), tokens)
        fetch_frame(f).wait()
        hidden[at, :] = normed(frames_ref[at, :].astype(F32), gain_s_ref[...]).astype(BF16)

    @pl.loop(0, parts)
    def _(c):
        fetch(c).wait()
        qkv[c] = jnp.dot(hidden[...], w_qkv[c], preferred_element_type=F32).astype(BF16)

    fetch_o.wait()
    third = parts // 3
    per = CHUNK // LANES

    @pl.loop(0, count)
    def _(f):
        at = pl.ds(pl.multiple_of(f * tokens, tokens), tokens)
        for pair in range(HEADS // 2):
            c, cols = pair // per, pl.ds((pair % per) * LANES, LANES)
            heads[:, pair * LANES : (pair + 1) * LANES] = head_pair(
                qkv[c, at, cols], qkv[third + c, at, cols], qkv[2 * third + c, at, cols], scale
            )
        update = jnp.dot(heads[...], w_o[...], preferred_element_type=F32)
        mixed = (frames_ref[at, :].astype(F32) + update).astype(BF16)
        mixed_ref[at, :] = mixed
        inner = normed(mixed.astype(F32), gain_t_ref[...])
        for i in range(2):
            for j in range(groups):
                stage[pl.ds(f * 2 * groups + i * groups + j, owners, stride=block), :] = inner[
                    i * owners : (i + 1) * owners, j * LANES : (j + 1) * LANES
                ]

    send_ref[...] = stage[...].astype(BF16)


def spatial(frames, gain_s, gain_t, w_qkv, w_o):
    count, tokens, width = frames.shape
    rows = count * tokens
    parts = 3 * width // CHUNK
    vmem = pl.BlockSpec(memory_space=pltpu.VMEM)
    hbm = pl.BlockSpec(memory_space=pl.ANY)
    return pl.pallas_call(
        functools.partial(spatial_kernel, tokens),
        out_shape=(
            jax.ShapeDtypeStruct((rows, width), BF16),
            jax.ShapeDtypeStruct((rows * width // LANES, LANES), BF16),
        ),
        in_specs=[hbm, vmem, vmem, hbm, hbm],
        out_specs=(vmem, vmem),
        scratch_shapes=[
            pltpu.VMEM((rows, width), BF16),
            pltpu.VMEM((parts, width, CHUNK), BF16),
            pltpu.VMEM((width, width), BF16),
            pltpu.VMEM((rows, width), BF16),
            pltpu.VMEM((parts, rows, CHUNK), BF16),
            pltpu.VMEM((tokens, width), BF16),
            pltpu.VMEM((rows * width // LANES, LANES), F32),
            pltpu.SemaphoreType.DMA((count,)),
            pltpu.SemaphoreType.DMA((parts,)),
            pltpu.SemaphoreType.DMA,
        ],
        compiler_params=pltpu.CompilerParams(vmem_limit_bytes=44 * 2**20),
        cost_estimate=pl.CostEstimate(flops=16 * 10**9, bytes_accessed=14 * 2**20, transcendentals=0),
        name="spatial",
    )(frames.reshape(rows, width), gain_s.reshape(1, width), gain_t.reshape(1, width), w_qkv, w_o)


def temporal_kernel(
    local_pos,
    len_ref,
    recv_ref,
    w_hbm,
    send_ref,
    w_qkv,
    w_o,
    hidden,
    qkv,
    heads,
    stage,
    cap,
    qkv_sem,
    o_sem,
):
    total = hidden.shape[0] // local_pos
    width = hidden.shape[1]
    parts = 3 * width // CHUNK
    scale = (width // HEADS) ** (-0.5)
    groups = width // LANES
    block = local_pos * groups
    span = cap.shape[1]

    def fetch(c):
        return pltpu.make_async_copy(
            w_hbm.at[:, pl.ds(pl.multiple_of(c * CHUNK, CHUNK), CHUNK)], w_qkv.at[c], qkv_sem.at[c]
        )

    fetch_o = pltpu.make_async_copy(w_hbm.at[:, pl.ds(3 * width, width)], w_o, o_sem)
    for c in range(parts):
        fetch(c).start()
    fetch_o.start()

    position = lax.broadcasted_iota(jnp.int32, (total, LANES), 0)

    def first(e, carry):
        end, begin = carry
        end = end + len_ref[e]
        return end, jnp.where(position >= end, end, begin)

    _, begin = lax.fori_loop(0, len_ref.shape[0], first, (jnp.int32(0), jnp.zeros((total, LANES), jnp.int32)))
    lane = lax.broadcasted_iota(jnp.int32, (span, LANES), 1)
    for b in range(total // span):
        rows = slice(b * span, (b + 1) * span)
        for side in range(2):
            other = lane + (b - 1 + side) * span
            fine = (other <= position[rows]) & (other >= begin[rows])
            cap[b, :, side * span : (side + 1) * span] = jnp.where(fine, jnp.inf, -1e30)

    stage[...] = recv_ref[...].astype(F32)
    for i in range(local_pos):
        for j in range(groups):
            hidden[i * total : (i + 1) * total, j * LANES : (j + 1) * LANES] = stage[
                pl.ds(i * groups + j, total, stride=block), :
            ].astype(BF16)

    @pl.loop(0, parts)
    def _(c):
        fetch(c).wait()
        qkv[c] = jnp.dot(hidden[...], w_qkv[c], preferred_element_type=F32).astype(BF16)

    fetch_o.wait()
    third = parts // 3
    per = CHUNK // LANES

    for i in range(local_pos):
        for b in range(total // span):
            at = pl.ds(i * total + b * span, span)
            low = max(b - 1, 0)
            seen = pl.ds(i * total + low * span, (b + 1 - low) * span)
            limit = cap[b] if b else cap[b, :, span:]
            for pair in range(HEADS // 2):
                c, cols = pair // per, pl.ds((pair % per) * LANES, LANES)
                heads[b * span : (b + 1) * span, pair * LANES : (pair + 1) * LANES] = head_pair(
                    qkv[c, at, cols], qkv[third + c, seen, cols], qkv[2 * third + c, seen, cols], scale, limit
                )
        update = jnp.dot(heads[...], w_o[...], preferred_element_type=F32)
        for j in range(groups):
            stage[pl.ds(i * groups + j, total, stride=block), :] = update[:, j * LANES : (j + 1) * LANES]

    send_ref[...] = stage[...].astype(BF16)


def temporal(episode_len, recv, weights, total, local_pos):
    width = weights.shape[0]
    rows = total * local_pos
    parts = 3 * width // CHUNK
    span = LANES
    vmem = pl.BlockSpec(memory_space=pltpu.VMEM)
    hbm = pl.BlockSpec(memory_space=pl.ANY)
    return pl.pallas_call(
        functools.partial(temporal_kernel, local_pos),
        out_shape=jax.ShapeDtypeStruct(recv.shape, BF16),
        in_specs=[pl.BlockSpec(memory_space=pltpu.SMEM), vmem, hbm],
        out_specs=vmem,
        scratch_shapes=[
            pltpu.VMEM((parts, width, CHUNK), BF16),
            pltpu.VMEM((width, width), BF16),
            pltpu.VMEM((rows, width), BF16),
            pltpu.VMEM((parts, rows, CHUNK), BF16),
            pltpu.VMEM((total, width), BF16),
            pltpu.VMEM((rows * width // LANES, LANES), F32),
            pltpu.VMEM((total // span, span, 2 * span), F32),
            pltpu.SemaphoreType.DMA((parts,)),
            pltpu.SemaphoreType.DMA,
        ],
        compiler_params=pltpu.CompilerParams(vmem_limit_bytes=44 * 2**20),
        cost_estimate=pl.CostEstimate(flops=16 * 10**9, bytes_accessed=14 * 2**20, transcendentals=0),
        name="temporal",
    )(episode_len, recv, weights)


def finish_kernel(tokens, mixed_ref, recv_ref, out_ref, stage):
    rows, width = mixed_ref.shape
    count = rows // tokens
    groups = width // LANES
    owners = tokens // 2
    block = count * 2 * groups
    stage[...] = recv_ref[...].astype(F32)
    for f in range(count):
        for i in range(2):
            for j in range(groups):
                at = (pl.ds(f * tokens + i * owners, owners), pl.ds(j * LANES, LANES))
                back = stage[pl.ds(f * 2 * groups + i * groups + j, owners, stride=block), :]
                out_ref[at] = (mixed_ref[at].astype(F32) + back).astype(BF16)


def finish(mixed, recv, tokens):
    vmem = pl.BlockSpec(memory_space=pltpu.VMEM)
    return pl.pallas_call(
        functools.partial(finish_kernel, tokens),
        out_shape=jax.ShapeDtypeStruct(mixed.shape, BF16),
        in_specs=[vmem, vmem],
        out_specs=vmem,
        scratch_shapes=[pltpu.VMEM(recv.shape, F32)],
        compiler_params=pltpu.CompilerParams(vmem_limit_bytes=32 * 2**20),
        name="finish",
    )(mixed, recv)


def local(frames, episode_len, norm_spatial, w_sqkv, w_so, norm_temporal, w_tqkv, w_to):
    axes = ("dp", "grp")
    count, tokens, width = frames.shape
    shards = lax.axis_size(axes)
    whole = lax.all_gather(jnp.concatenate([w_tqkv, w_to], axis=1), axes, axis=0, tiled=True)
    mixed, send = spatial(frames, norm_spatial, norm_temporal, w_sqkv, w_so)
    block = (shards, -1, LANES)
    recv = lax.all_to_all(send.reshape(block), axes, split_axis=0, concat_axis=0, tiled=True)
    back = temporal(
        episode_len, recv.reshape(-1, LANES), whole, count * shards, tokens // shards
    )
    returned = lax.all_to_all(back.reshape(block), axes, split_axis=0, concat_axis=0, tiled=True)
    return finish(mixed, returned.reshape(-1, LANES), tokens).reshape(frames.shape)


def solution(mesh):
    placed = (
        P(("dp", "grp"), None, None),
        P(),
        P(),
        P(),
        P(),
        P(),
        P(("dp", "grp"), None),
        P(("dp", "grp"), None),
    )
    return jax.shard_map(
        local, mesh=mesh, in_specs=placed, out_specs=P(("dp", "grp"), None, None), check_vma=False
    )
```

```python
import functools

import jax
import jax.numpy as jnp
from jax import lax
from jax.experimental import pallas as pl
from jax.experimental.pallas import tpu as pltpu
from jax.sharding import PartitionSpec as P

HEADS = 16
LANES = 128
CHUNK = 256
TOGETHER = 3
LOG2E = 1.4426950408889634
F32 = jnp.float32
BF16 = jnp.bfloat16


def normed(wide, gain):
    scale = lax.rsqrt(jnp.mean(wide * wide, axis=-1, keepdims=True) + 1e-06)
    return wide * scale * gain


def head_pair(q2, k2, v2, scale, cap=None):
    lane = lax.broadcasted_iota(jnp.int32, q2.shape, 1)
    zero = jnp.zeros_like(q2)
    outs = []
    for side in range(2):
        mine = lane < 64 if side == 0 else lane >= 64
        q = jnp.where(mine, q2, zero)
        scores = lax.dot_general(q, k2, (((1,), (1,)), ((), ())), preferred_element_type=F32)
        if cap is not None:
            scores = jnp.minimum(scores, cap)
        top = jnp.max(scores, axis=-1, keepdims=True)
        weights = jnp.exp2((scores - top) * (scale * LOG2E))
        total = jnp.sum(weights, axis=-1, keepdims=True)
        out = jnp.dot(weights.astype(BF16), v2, preferred_element_type=F32)
        outs.append(out * (1.0 / total))
    return jnp.where(lane < 64, outs[0], outs[1]).astype(BF16)


def spatial_kernel(
    tokens,
    frames_hbm,
    gain_s_hbm,
    gain_t_hbm,
    w_qkv_hbm,
    w_o_hbm,
    mixed_ref,
    send_ref,
    frames_ref,
    gain_s_ref,
    gain_t_ref,
    w_qkv,
    w_o,
    hidden,
    qkv,
    heads,
    stage,
    gain_sem,
    frame_sem,
    qkv_sem,
    o_sem,
):
    rows, width = frames_ref.shape
    count = rows // tokens
    parts = 3 * width // CHUNK
    scale = (width // HEADS) ** (-0.5)
    groups = width // LANES
    owners = tokens // 2
    block = count * 2 * groups

    def fetch(c):
        return pltpu.make_async_copy(
            w_qkv_hbm.at[:, pl.ds(pl.multiple_of(c * CHUNK, CHUNK), CHUNK)], w_qkv.at[c], qkv_sem.at[c]
        )

    fetch_o = pltpu.make_async_copy(w_o_hbm, w_o, o_sem)

    def fetch_frame(f):
        at = pl.ds(pl.multiple_of(f * tokens, tokens), tokens)
        return pltpu.make_async_copy(frames_hbm.at[at, :], frames_ref.at[at, :], frame_sem.at[f])

    gains = (
        pltpu.make_async_copy(gain_s_hbm, gain_s_ref, gain_sem.at[0]),
        pltpu.make_async_copy(gain_t_hbm, gain_t_ref, gain_sem.at[1]),
    )
    for copy in gains:
        copy.start()
    for f in range(count):
        fetch_frame(f).start()
    for c in range(parts):
        fetch(c).start()
    fetch_o.start()
    for copy in gains:
        copy.wait()

    @pl.loop(0, count)
    def _(f):
        at = pl.ds(pl.multiple_of(f * tokens, tokens), tokens)
        fetch_frame(f).wait()
        hidden[at, :] = normed(frames_ref[at, :].astype(F32), gain_s_ref[...]).astype(BF16)

    @pl.loop(0, parts, step=TOGETHER)
    def _(first):
        for c in range(TOGETHER):
            fetch(first + c).wait()
        for c in range(TOGETHER):
            qkv[first + c] = jnp.dot(hidden[...], w_qkv[first + c], preferred_element_type=F32).astype(BF16)

    fetch_o.wait()
    third = parts // 3
    per = CHUNK // LANES

    @pl.loop(0, count)
    def _(f):
        at = pl.ds(pl.multiple_of(f * tokens, tokens), tokens)
        for pair in range(HEADS // 2):
            c, cols = pair // per, pl.ds((pair % per) * LANES, LANES)
            heads[:, pair * LANES : (pair + 1) * LANES] = head_pair(
                qkv[c, at, cols], qkv[third + c, at, cols], qkv[2 * third + c, at, cols], scale
            )
        update = jnp.dot(heads[...], w_o[...], preferred_element_type=F32)
        mixed = (frames_ref[at, :].astype(F32) + update).astype(BF16)
        mixed_ref[at, :] = mixed
        inner = normed(mixed.astype(F32), gain_t_ref[...])
        for i in range(2):
            for j in range(groups):
                stage[pl.ds(f * 2 * groups + i * groups + j, owners, stride=block), :] = inner[
                    i * owners : (i + 1) * owners, j * LANES : (j + 1) * LANES
                ]

    send_ref[...] = stage[...].astype(BF16)


def spatial(frames, gain_s, gain_t, w_qkv, w_o):
    count, tokens, width = frames.shape
    rows = count * tokens
    parts = 3 * width // CHUNK
    vmem = pl.BlockSpec(memory_space=pltpu.VMEM)
    hbm = pl.BlockSpec(memory_space=pltpu.HBM)
    return pl.pallas_call(
        functools.partial(spatial_kernel, tokens),
        out_shape=(
            jax.ShapeDtypeStruct((rows, width), BF16),
            jax.ShapeDtypeStruct((rows * width // LANES, LANES), BF16),
        ),
        in_specs=[hbm] * 5,
        out_specs=(vmem, vmem),
        scratch_shapes=[
            pltpu.VMEM((rows, width), BF16),
            pltpu.VMEM((1, width), F32),
            pltpu.VMEM((1, width), F32),
            pltpu.VMEM((parts, width, CHUNK), BF16),
            pltpu.VMEM((width, width), BF16),
            pltpu.VMEM((rows, width), BF16),
            pltpu.VMEM((parts, rows, CHUNK), BF16),
            pltpu.VMEM((tokens, width), BF16),
            pltpu.VMEM((rows * width // LANES, LANES), F32),
            pltpu.SemaphoreType.DMA((2,)),
            pltpu.SemaphoreType.DMA((count,)),
            pltpu.SemaphoreType.DMA((parts,)),
            pltpu.SemaphoreType.DMA,
        ],
        compiler_params=pltpu.CompilerParams(vmem_limit_bytes=44 * 2**20),
        cost_estimate=pl.CostEstimate(flops=16 * 10**9, bytes_accessed=14 * 2**20, transcendentals=0),
        name="spatial",
    )(frames.reshape(rows, width), gain_s.reshape(1, width), gain_t.reshape(1, width), w_qkv, w_o)


def temporal_kernel(
    local_pos,
    len_ref,
    recv_ref,
    w_hbm,
    send_ref,
    w_qkv,
    w_o,
    hidden,
    qkv,
    heads,
    stage,
    cap,
    qkv_sem,
    o_sem,
):
    total = hidden.shape[0] // local_pos
    width = hidden.shape[1]
    parts = 3 * width // CHUNK
    scale = (width // HEADS) ** (-0.5)
    groups = width // LANES
    block = local_pos * groups
    span, seen = cap.shape[1:]
    back = total - seen

    def fetch(c):
        return pltpu.make_async_copy(
            w_hbm.at[:, pl.ds(pl.multiple_of(c * CHUNK, CHUNK), CHUNK)], w_qkv.at[c], qkv_sem.at[c]
        )

    fetch_o = pltpu.make_async_copy(w_hbm.at[:, pl.ds(3 * width, width)], w_o, o_sem)
    for c in range(parts):
        fetch(c).start()
    fetch_o.start()

    position = lax.broadcasted_iota(jnp.int32, (total, LANES), 0)

    def first(e, carry):
        end, begin = carry
        end = end + len_ref[e]
        return end, jnp.where(position >= end, end, begin)

    _, begin = lax.fori_loop(0, len_ref.shape[0], first, (jnp.int32(0), jnp.zeros((total, LANES), jnp.int32)))
    lane = lax.broadcasted_iota(jnp.int32, (span, LANES), 1)
    for b in range(total // span):
        rows = slice(b * span, (b + 1) * span)
        for side in range(seen // LANES):
            other = lane + b * back + side * LANES
            fine = (other <= position[rows]) & (other >= begin[rows])
            cap[b, :, side * LANES : (side + 1) * LANES] = jnp.where(fine, jnp.inf, -1e30)

    stage[...] = recv_ref[...].astype(F32)
    for i in range(local_pos):
        for j in range(groups):
            hidden[i * total : (i + 1) * total, j * LANES : (j + 1) * LANES] = stage[
                pl.ds(i * groups + j, total, stride=block), :
            ].astype(BF16)

    @pl.loop(0, parts, step=TOGETHER)
    def _(first):
        for c in range(TOGETHER):
            fetch(first + c).wait()
        for c in range(TOGETHER):
            qkv[first + c] = jnp.dot(hidden[...], w_qkv[first + c], preferred_element_type=F32).astype(BF16)

    fetch_o.wait()
    third = parts // 3
    per = CHUNK // LANES

    @pl.loop(0, local_pos)
    def _(i):
        @pl.loop(0, total // span)
        def _(b):
            at = pl.ds(pl.multiple_of(i * total + b * span, LANES // 2), span)
            near = pl.ds(pl.multiple_of(i * total + b * back, LANES), seen)
            limit = cap[b]
            for pair in range(HEADS // 2):
                c, cols = pair // per, pl.ds((pair % per) * LANES, LANES)
                heads[pl.ds(pl.multiple_of(b * span, LANES // 2), span), pl.ds(pair * LANES, LANES)] = head_pair(
                    qkv[c, at, cols], qkv[third + c, near, cols], qkv[2 * third + c, near, cols], scale, limit
                )

        update = jnp.dot(heads[...], w_o[...], preferred_element_type=F32)
        for j in range(groups):
            stage[pl.ds(i * groups + j, total, stride=block), :] = update[:, j * LANES : (j + 1) * LANES]

    send_ref[...] = stage[...].astype(BF16)


def temporal(episode_len, recv, weights, total, local_pos):
    width = weights.shape[0]
    rows = total * local_pos
    parts = 3 * width // CHUNK
    span, seen = total // 2, 2 * LANES
    vmem = pl.BlockSpec(memory_space=pltpu.VMEM)
    hbm = pl.BlockSpec(memory_space=pl.ANY)
    return pl.pallas_call(
        functools.partial(temporal_kernel, local_pos),
        out_shape=jax.ShapeDtypeStruct(recv.shape, BF16),
        in_specs=[pl.BlockSpec(memory_space=pltpu.SMEM), vmem, hbm],
        out_specs=vmem,
        scratch_shapes=[
            pltpu.VMEM((parts, width, CHUNK), BF16),
            pltpu.VMEM((width, width), BF16),
            pltpu.VMEM((rows, width), BF16),
            pltpu.VMEM((parts, rows, CHUNK), BF16),
            pltpu.VMEM((total, width), BF16),
            pltpu.VMEM((rows * width // LANES, LANES), F32),
            pltpu.VMEM((total // span, span, seen), F32),
            pltpu.SemaphoreType.DMA((parts,)),
            pltpu.SemaphoreType.DMA,
        ],
        compiler_params=pltpu.CompilerParams(vmem_limit_bytes=44 * 2**20),
        cost_estimate=pl.CostEstimate(flops=16 * 10**9, bytes_accessed=14 * 2**20, transcendentals=0),
        name="temporal",
    )(episode_len, recv, weights)


def finish_kernel(tokens, mixed_ref, recv_ref, out_ref, stage):
    rows, width = mixed_ref.shape
    count = rows // tokens
    groups = width // LANES
    owners = tokens // 2
    block = count * 2 * groups
    stage[...] = recv_ref[...].astype(F32)
    for f in range(count):
        for i in range(2):
            for j in range(groups):
                at = (pl.ds(f * tokens + i * owners, owners), pl.ds(j * LANES, LANES))
                back = stage[pl.ds(f * 2 * groups + i * groups + j, owners, stride=block), :]
                out_ref[at] = (mixed_ref[at].astype(F32) + back).astype(BF16)


def finish(mixed, recv, tokens):
    vmem = pl.BlockSpec(memory_space=pltpu.VMEM)
    return pl.pallas_call(
        functools.partial(finish_kernel, tokens),
        out_shape=jax.ShapeDtypeStruct(mixed.shape, BF16),
        in_specs=[vmem, vmem],
        out_specs=vmem,
        scratch_shapes=[pltpu.VMEM(recv.shape, F32)],
        compiler_params=pltpu.CompilerParams(vmem_limit_bytes=32 * 2**20),
        name="finish",
    )(mixed, recv)


def local(frames, episode_len, norm_spatial, w_sqkv, w_so, norm_temporal, w_tqkv, w_to):
    axes = ("dp", "grp")
    count, tokens, width = frames.shape
    shards = lax.axis_size(axes)
    whole = lax.all_gather(jnp.concatenate([w_tqkv, w_to], axis=1), axes, axis=0, tiled=True)
    mixed, send = spatial(frames, norm_spatial, norm_temporal, w_sqkv, w_so)
    block = (shards, -1, LANES)
    recv = lax.all_to_all(send.reshape(block), axes, split_axis=0, concat_axis=0, tiled=True)
    back = temporal(
        episode_len, recv.reshape(-1, LANES), whole, count * shards, tokens // shards
    )
    returned = lax.all_to_all(back.reshape(block), axes, split_axis=0, concat_axis=0, tiled=True)
    return finish(mixed, returned.reshape(-1, LANES), tokens).reshape(frames.shape)


def solution(mesh):
    placed = (
        P(("dp", "grp"), None, None),
        P(),
        P(),
        P(),
        P(),
        P(),
        P(("dp", "grp"), None),
        P(("dp", "grp"), None),
    )
    return jax.shard_map(
        local, mesh=mesh, in_specs=placed, out_specs=P(("dp", "grp"), None, None), check_vma=False
    )
```

```python
import functools

import jax
import jax.numpy as jnp
from jax import lax
from jax.experimental import pallas as pl
from jax.experimental.pallas import tpu as pltpu
from jax.sharding import PartitionSpec as P

HEADS = 16
LANES = 128
CHUNK = 256
TOGETHER = 3
LOG2E = 1.4426950408889634
F32 = jnp.float32
BF16 = jnp.bfloat16


def normed(wide, gain):
    scale = lax.rsqrt(jnp.mean(wide * wide, axis=-1, keepdims=True) + 1e-06)
    return wide * scale * gain


def head_pair(q2, k2, v2, scale, cap=None):
    lane = lax.broadcasted_iota(jnp.int32, q2.shape, 1)
    zero = jnp.zeros_like(q2)
    outs = []
    for side in range(2):
        mine = lane < 64 if side == 0 else lane >= 64
        q = jnp.where(mine, q2, zero)
        scores = lax.dot_general(q, k2, (((1,), (1,)), ((), ())), preferred_element_type=F32)
        if cap is not None:
            scores = jnp.minimum(scores, cap)
        top = jnp.max(scores, axis=-1, keepdims=True)
        weights = jnp.exp2((scores - top) * (scale * LOG2E))
        total = jnp.sum(weights, axis=-1, keepdims=True)
        out = jnp.dot(weights.astype(BF16), v2, preferred_element_type=F32)
        outs.append(out * (1.0 / total))
    return jnp.where(lane < 64, outs[0], outs[1]).astype(BF16)


def spatial_kernel(
    tokens,
    frames_hbm,
    gain_s_hbm,
    gain_t_hbm,
    w_qkv_hbm,
    w_o_hbm,
    mixed_ref,
    send_ref,
    frames_ref,
    gain_s_ref,
    gain_t_ref,
    w_qkv,
    w_o,
    hidden,
    qkv,
    heads,
    gain_sem,
    frame_sem,
    qkv_sem,
    o_sem,
):
    rows, width = frames_ref.shape
    count = rows // tokens
    parts = 3 * width // CHUNK
    scale = (width // HEADS) ** (-0.5)
    groups = width // LANES
    owners = tokens // 2

    def fetch(c):
        return pltpu.make_async_copy(
            w_qkv_hbm.at[:, pl.ds(pl.multiple_of(c * CHUNK, CHUNK), CHUNK)], w_qkv.at[c], qkv_sem.at[c]
        )

    fetch_o = pltpu.make_async_copy(w_o_hbm, w_o, o_sem)

    def fetch_frame(f):
        at = pl.ds(pl.multiple_of(f * tokens, tokens), tokens)
        return pltpu.make_async_copy(frames_hbm.at[at, :], frames_ref.at[at, :], frame_sem.at[f])

    gains = (
        pltpu.make_async_copy(gain_s_hbm, gain_s_ref, gain_sem.at[0]),
        pltpu.make_async_copy(gain_t_hbm, gain_t_ref, gain_sem.at[1]),
    )
    for copy in gains:
        copy.start()
    for f in range(count):
        fetch_frame(f).start()
    for c in range(parts):
        fetch(c).start()
    fetch_o.start()
    for copy in gains:
        copy.wait()

    @pl.loop(0, count)
    def _(f):
        at = pl.ds(pl.multiple_of(f * tokens, tokens), tokens)
        fetch_frame(f).wait()
        hidden[at, :] = normed(frames_ref[at, :].astype(F32), gain_s_ref[...]).astype(BF16)

    @pl.loop(0, parts, step=TOGETHER)
    def _(first):
        for c in range(TOGETHER):
            fetch(first + c).wait()
        for c in range(TOGETHER):
            qkv[first + c] = jnp.dot(hidden[...], w_qkv[first + c], preferred_element_type=F32).astype(BF16)

    fetch_o.wait()
    third = parts // 3
    per = CHUNK // LANES

    @pl.loop(0, count)
    def _(f):
        at = pl.ds(pl.multiple_of(f * tokens, tokens), tokens)
        for pair in range(HEADS // 2):
            c, cols = pair // per, pl.ds((pair % per) * LANES, LANES)
            heads[:, pair * LANES : (pair + 1) * LANES] = head_pair(
                qkv[c, at, cols], qkv[third + c, at, cols], qkv[2 * third + c, at, cols], scale
            )
        update = jnp.dot(heads[...], w_o[...], preferred_element_type=F32)
        mixed = (frames_ref[at, :].astype(F32) + update).astype(BF16)
        mixed_ref[at, :] = mixed
        inner = normed(mixed.astype(F32), gain_t_ref[...])
        both = [inner[i * owners : (i + 1) * owners].reshape(owners, groups, LANES) for i in range(2)]
        rows_out = pl.ds(pl.multiple_of(f * 2 * groups, 2 * groups), 2 * groups)
        send_ref[:, rows_out, :] = jnp.concatenate(both, axis=1).astype(BF16)


def spatial(frames, gain_s, gain_t, w_qkv, w_o):
    count, tokens, width = frames.shape
    rows = count * tokens
    parts = 3 * width // CHUNK
    vmem = pl.BlockSpec(memory_space=pltpu.VMEM)
    hbm = pl.BlockSpec(memory_space=pltpu.HBM)
    return pl.pallas_call(
        functools.partial(spatial_kernel, tokens),
        out_shape=(
            jax.ShapeDtypeStruct((rows, width), BF16),
            jax.ShapeDtypeStruct((tokens // 2, count * 2 * width // LANES, LANES), BF16),
        ),
        in_specs=[hbm] * 5,
        out_specs=(vmem, vmem),
        scratch_shapes=[
            pltpu.VMEM((rows, width), BF16),
            pltpu.VMEM((1, width), F32),
            pltpu.VMEM((1, width), F32),
            pltpu.VMEM((parts, width, CHUNK), BF16),
            pltpu.VMEM((width, width), BF16),
            pltpu.VMEM((rows, width), BF16),
            pltpu.VMEM((parts, rows, CHUNK), BF16),
            pltpu.VMEM((tokens, width), BF16),
            pltpu.SemaphoreType.DMA((2,)),
            pltpu.SemaphoreType.DMA((count,)),
            pltpu.SemaphoreType.DMA((parts,)),
            pltpu.SemaphoreType.DMA,
        ],
        compiler_params=pltpu.CompilerParams(vmem_limit_bytes=44 * 2**20),
        cost_estimate=pl.CostEstimate(flops=16 * 10**9, bytes_accessed=14 * 2**20, transcendentals=0),
        name="spatial",
    )(frames.reshape(rows, width), gain_s.reshape(1, width), gain_t.reshape(1, width), w_qkv, w_o)


def temporal_kernel(
    local_pos,
    len_ref,
    recv_ref,
    *refs,
):
    parts_in, (send_ref, w_qkv, hidden, qkv, heads, cap) = refs[:-6], refs[-6:]
    total = hidden.shape[0] // local_pos
    width = hidden.shape[1]
    parts = 3 * width // CHUNK
    scale = (width // HEADS) ** (-0.5)
    groups = width // LANES
    block = local_pos * groups
    span, seen = cap.shape[1:]
    back = total - seen

    position = lax.broadcasted_iota(jnp.int32, (total, LANES), 0)

    def first(e, carry):
        end, begin = carry
        end = end + len_ref[e]
        return end, jnp.where(position >= end, end, begin)

    _, begin = lax.fori_loop(0, len_ref.shape[0], first, (jnp.int32(0), jnp.zeros((total, LANES), jnp.int32)))
    lane = lax.broadcasted_iota(jnp.int32, (span, LANES), 1)
    for b in range(total // span):
        rows = slice(b * span, (b + 1) * span)
        for side in range(seen // LANES):
            other = lane + b * back + side * LANES
            fine = (other <= position[rows]) & (other >= begin[rows])
            cap[b, :, side * LANES : (side + 1) * LANES] = jnp.where(fine, jnp.inf, -1e30)

    step = 4 * groups
    for k in range(total // step):
        wide = recv_ref[pl.ds(k * step * block, step * block), :].astype(F32)
        wide = wide.reshape(step, local_pos, groups, LANES)
        for i in range(local_pos):
            at = i * total + k * step
            hidden[at : at + step, :] = wide[:, i].reshape(step, width).astype(BF16)

    lines = w_qkv.shape[1]
    put_rows(parts_in, (0, 1, 3, 2, 2), (0, 0, 0, 0, lines // 2), w_qkv)

    @pl.loop(0, parts, step=TOGETHER)
    def _(first):
        for c in range(TOGETHER):
            weights = w_qkv[first + c].reshape(width, CHUNK)
            qkv[first + c] = jnp.dot(hidden[...], weights, preferred_element_type=F32).astype(BF16)

    third = parts // 3
    per = CHUNK // LANES

    @pl.loop(0, local_pos)
    def _(i):
        @pl.loop(0, total // span)
        def _(b):
            at = pl.ds(pl.multiple_of(i * total + b * span, LANES // 2), span)
            near = pl.ds(pl.multiple_of(i * total + b * back, LANES), seen)
            limit = cap[b]
            for pair in range(HEADS // 2):
                c, cols = pair // per, pl.ds((pair % per) * LANES, LANES)
                heads[at, pl.ds(pair * LANES, LANES)] = head_pair(
                    qkv[c, at, cols], qkv[third + c, near, cols], qkv[2 * third + c, near, cols], scale, limit
                )

    for k in range(total // step):
        both = [
            heads[i * total + k * step : i * total + (k + 1) * step, :].astype(F32).reshape(step, groups, LANES)
            for i in range(local_pos)
        ]
        wide = jnp.stack(both, axis=1).reshape(step * block, LANES)
        send_ref[pl.ds(k * step * block, step * block), :] = wide.astype(BF16)


def temporal(episode_len, recv, weights, total, local_pos):
    lines, rows, cols = weights[0].shape
    width = lines * SIDE * rows
    tokens = total * local_pos
    parts = 3 * width // CHUNK
    span, seen = total // 2, 2 * LANES
    vmem = pl.BlockSpec(memory_space=pltpu.VMEM)
    return pl.pallas_call(
        functools.partial(temporal_kernel, local_pos),
        out_shape=jax.ShapeDtypeStruct(recv.shape, BF16),
        in_specs=[pl.BlockSpec(memory_space=pltpu.SMEM)] + [vmem] * (1 + len(weights)),
        out_specs=vmem,
        scratch_shapes=[
            pltpu.VMEM((parts, lines, SIDE, rows, CHUNK), BF16),
            pltpu.VMEM((tokens, width), BF16),
            pltpu.VMEM((parts, tokens, CHUNK), BF16),
            pltpu.VMEM((tokens, width), BF16),
            pltpu.VMEM((total // span, span, seen), F32),
        ],
        compiler_params=pltpu.CompilerParams(vmem_limit_bytes=32 * 2**20),
        cost_estimate=pl.CostEstimate(flops=16 * 10**9, bytes_accessed=14 * 2**20, transcendentals=0),
        name="temporal",
    )(episode_len, recv, *weights)


def finish_kernel(tokens, mixed_ref, recv_ref, *refs):
    parts_in, (out_ref, w_o, heads) = refs[:-3], refs[-3:]
    rows, width = mixed_ref.shape
    count = rows // tokens
    groups = width // LANES
    owners = tokens // 2
    put_rows(parts_in, (0, 1, 3, 2), (0, 0, 0, 0), w_o)
    for f in range(count):
        wide = recv_ref[:, f * 2 * groups : (f + 1) * 2 * groups, :].astype(F32)
        wide = wide.reshape(owners, 2, groups, LANES)
        for i in range(2):
            at = f * tokens + i * owners
            heads[at : at + owners, :] = wide[:, i].reshape(owners, width).astype(BF16)
    for c in range(width // CHUNK):
        cols = pl.ds(c * CHUNK, CHUNK)
        weights = w_o[c].reshape(width, CHUNK)
        update = jnp.dot(heads[...], weights, preferred_element_type=F32).astype(BF16)
        out_ref[:, cols] = (mixed_ref[:, cols].astype(F32) + update.astype(F32)).astype(BF16)


def finish(mixed, recv, weights, tokens):
    lines, rows, cols = weights[0].shape
    vmem = pl.BlockSpec(memory_space=pltpu.VMEM)
    return pl.pallas_call(
        functools.partial(finish_kernel, tokens),
        out_shape=jax.ShapeDtypeStruct(mixed.shape, BF16),
        in_specs=[vmem] * (2 + len(weights)),
        out_specs=vmem,
        scratch_shapes=[
            pltpu.VMEM((2 * cols // CHUNK, lines, SIDE, rows, CHUNK), BF16),
            pltpu.VMEM(mixed.shape, BF16),
        ],
        compiler_params=pltpu.CompilerParams(vmem_limit_bytes=24 * 2**20),
        cost_estimate=pl.CostEstimate(flops=2 * 10**9, bytes_accessed=6 * 2**20, transcendentals=0),
        name="finish",
    )(mixed, recv, *weights)


AXES = ("dp", "grp")
SIDE = 4


def device(z, y, x, core):
    return ((z * SIDE + y) * SIDE + x % SIDE) * 2 + core


def swap_halves(shard):
    span = range(SIDE)
    pairs = [[device(z, y, x, 0), device(z, y, x, 1)] for z in span for y in span for x in span]
    return lax.all_to_all(shard, AXES, split_axis=1, concat_axis=0, tiled=True, axis_index_groups=pairs)


def spread(block):
    span = range(SIDE)
    planes = [[device(z, y, x, core) for z in span for y in span] for x in span for core in range(2)]
    copies = jnp.broadcast_to(block[None], (len(planes[0]),) + block.shape)
    return lax.all_to_all(copies, AXES, split_axis=0, concat_axis=0, tiled=True, axis_index_groups=planes)


def along_x(part, step):
    span = range(SIDE)
    places = [(z, y, x, core) for z in span for y in span for x in span for core in range(2)]
    pairs = [(device(z, y, x, core), device(z, y, x + step, core)) for z, y, x, core in places]
    return lax.ppermute(part, AXES, pairs)


def from_sibling(part):
    count = lax.axis_size(AXES)
    return lax.ppermute(part, AXES, [(k, k ^ 1) for k in range(count)])


def put_rows(parts, shifts, lows, blocks):
    x = lax.axis_index("grp") // 2
    core = lax.rem(lax.axis_index("grp"), 2)
    half = blocks.shape[0] // 2
    count = len(shifts)
    for k, part in enumerate(parts):
        side = core if k < count else 1 - core
        origin = lax.rem(x + SIDE - shifts[k % count], SIDE)
        low = lows[k % count]
        for line in range(part.shape[0]):
            for c in range(half):
                blocks[side * half + c, low + line, origin] = part[line, :, c * CHUNK : (c + 1) * CHUNK]


def exchange(array, shards):
    blocks = array.reshape(shards, -1, LANES)
    return lax.all_to_all(blocks, AXES, split_axis=0, concat_axis=0, tiled=True)


def local(frames, episode_len, norm_spatial, w_sqkv, w_so, norm_temporal, w_tqkv, w_to):
    count, tokens, width = frames.shape
    shards = lax.axis_size(AXES)
    cut = 3 * width // 2
    halves = [w_tqkv[:, :cut], w_to[:, : width // 2], w_tqkv[:, cut:], w_to[:, width // 2 :]]
    plane = spread(swap_halves(jnp.concatenate(halves, axis=1)))
    mixed, send = spatial(frames, norm_spatial, norm_temporal, w_sqkv, w_so)
    plane, send = lax.optimization_barrier((plane, send))
    own, own_o = plane[:, :, :cut], plane[:, :, cut:]
    left, right = along_x(own, 1), along_x(own, -1)
    lines = plane.shape[0]
    mine = [own, left, right, along_x(left[: lines // 2], 1), along_x(right[lines // 2 :], -1)]
    theirs = [from_sibling(part) for part in mine]
    recv = exchange(send, shards)
    recv, own_o = lax.optimization_barrier((recv, own_o))
    mine_o = [own_o] + [along_x(own_o, step) for step in (1, -1, 2)]
    back = temporal(episode_len, recv.reshape(-1, LANES), mine + theirs, count * shards, tokens // shards)
    back, mine_o = lax.optimization_barrier((back, mine_o))
    theirs_o = [from_sibling(part) for part in mine_o]
    returned = exchange(back, shards)
    return finish(mixed, returned, mine_o + theirs_o, tokens).reshape(frames.shape)


def solution(mesh):
    placed = (
        P(("dp", "grp"), None, None),
        P(),
        P(),
        P(),
        P(),
        P(),
        P(("dp", "grp"), None),
        P(("dp", "grp"), None),
    )
    return jax.shard_map(
        local, mesh=mesh, in_specs=placed, out_specs=P(("dp", "grp"), None, None), check_vma=False
    )
```

```python
import functools

import jax
import jax.numpy as jnp
from jax import lax
from jax.experimental import pallas as pl
from jax.experimental.pallas import tpu as pltpu
from jax.sharding import PartitionSpec as P

HEADS = 16
LANES = 128
CHUNK = 256
TOGETHER = 3
VMEM = 63 * 10**6
LOG2E = 1.4426950408889634
F32 = jnp.float32
BF16 = jnp.bfloat16


def normed(wide, gain):
    scale = lax.rsqrt(jnp.mean(wide * wide, axis=-1, keepdims=True) + 1e-06)
    return wide * scale * gain


def head_pair(q2, k2, v2, scale, cap=None):
    lane = lax.broadcasted_iota(jnp.int32, q2.shape, 1)
    zero = jnp.zeros_like(q2)
    outs = []
    for side in range(2):
        mine = lane < 64 if side == 0 else lane >= 64
        q = jnp.where(mine, q2, zero)
        scores = lax.dot_general(q, k2, (((1,), (1,)), ((), ())), preferred_element_type=F32)
        if cap is not None:
            scores = jnp.minimum(scores, cap)
        top = jnp.max(scores, axis=-1, keepdims=True)
        weights = jnp.exp2((scores - top) * (scale * LOG2E))
        total = jnp.sum(weights, axis=-1, keepdims=True)
        out = jnp.dot(weights.astype(BF16), v2, preferred_element_type=F32)
        outs.append(out * (1.0 / total))
    return jnp.where(lane < 64, outs[0], outs[1]).astype(BF16)


def spatial_kernel(
    tokens,
    frames_hbm,
    gain_s_hbm,
    gain_t_hbm,
    w_qkv_hbm,
    w_o_hbm,
    mixed_hbm,
    send_hbm,
    mixed_ref,
    send_ref,
    frames_ref,
    gain_s_ref,
    gain_t_ref,
    w_qkv,
    w_o,
    hidden,
    qkv,
    heads,
    gain_sem,
    frame_sem,
    qkv_sem,
    o_sem,
    mixed_sem,
    send_sem,
):
    rows, width = frames_ref.shape
    count = rows // tokens
    parts = 3 * width // CHUNK
    scale = (width // HEADS) ** (-0.5)
    groups = width // LANES
    owners = tokens // 2

    def fetch(c):
        return pltpu.make_async_copy(
            w_qkv_hbm.at[:, pl.ds(pl.multiple_of(c * CHUNK, CHUNK), CHUNK)], w_qkv.at[c], qkv_sem.at[c]
        )

    fetch_o = pltpu.make_async_copy(w_o_hbm, w_o, o_sem)

    def fetch_frame(f):
        at = pl.ds(pl.multiple_of(f * tokens, tokens), tokens)
        return pltpu.make_async_copy(frames_hbm.at[at, :], frames_ref.at[at, :], frame_sem.at[f])

    def give_mixed(f):
        at = pl.ds(pl.multiple_of(f * tokens, tokens), tokens)
        return pltpu.make_async_copy(mixed_ref.at[at, :], mixed_hbm.at[at, :], mixed_sem.at[f])

    def give_send(f):
        at = pl.ds(pl.multiple_of(f * 2 * groups, 2 * groups), 2 * groups)
        return pltpu.make_async_copy(send_ref.at[:, at, :], send_hbm.at[:, at, :], send_sem.at[f])

    gains = (
        pltpu.make_async_copy(gain_s_hbm, gain_s_ref, gain_sem.at[0]),
        pltpu.make_async_copy(gain_t_hbm, gain_t_ref, gain_sem.at[1]),
    )
    for copy in gains:
        copy.start()
    for f in range(count):
        fetch_frame(f).start()
    for copy in gains:
        copy.wait()

    @pl.loop(0, count)
    def _(f):
        at = pl.ds(pl.multiple_of(f * tokens, tokens), tokens)
        fetch_frame(f).wait()
        for c in range(parts // 4):
            fetch(f * (parts // 4) + c).start()
        hidden[at, :] = normed(frames_ref[at, :].astype(F32), gain_s_ref[...]).astype(BF16)

    for c in range(count * (parts // 4), parts):
        fetch(c).start()
    fetch_o.start()

    @pl.loop(0, parts, step=TOGETHER)
    def _(first):
        for c in range(TOGETHER):
            fetch(first + c).wait()
        for c in range(TOGETHER):
            qkv[first + c] = jnp.dot(hidden[...], w_qkv[first + c], preferred_element_type=F32).astype(BF16)

    fetch_o.wait()
    third = parts // 3
    per = CHUNK // LANES

    @pl.loop(0, count)
    def _(f):
        at = pl.ds(pl.multiple_of(f * tokens, tokens), tokens)
        for pair in range(HEADS // 2):
            c, cols = pair // per, pl.ds((pair % per) * LANES, LANES)
            heads[:, pair * LANES : (pair + 1) * LANES] = head_pair(
                qkv[c, at, cols], qkv[third + c, at, cols], qkv[2 * third + c, at, cols], scale
            )
        update = jnp.dot(heads[...], w_o[...], preferred_element_type=F32)
        mixed = (frames_ref[at, :].astype(F32) + update).astype(BF16)
        mixed_ref[at, :] = mixed
        inner = normed(mixed.astype(F32), gain_t_ref[...])
        both = [inner[i * owners : (i + 1) * owners].reshape(owners, groups, LANES) for i in range(2)]
        rows_out = pl.ds(pl.multiple_of(f * 2 * groups, 2 * groups), 2 * groups)
        send_ref[:, rows_out, :] = jnp.concatenate(both, axis=1).astype(BF16)
        give_mixed(f).start()
        give_send(f).start()

    for f in range(count):
        give_mixed(f).wait()
        give_send(f).wait()


def spatial(frames, gain_s, gain_t, w_qkv, w_o):
    count, tokens, width = frames.shape
    rows = count * tokens
    parts = 3 * width // CHUNK
    blocks = (tokens // 2, count * 2 * width // LANES, LANES)
    hbm = pl.BlockSpec(memory_space=pl.ANY)
    return pl.pallas_call(
        functools.partial(spatial_kernel, tokens),
        out_shape=(
            jax.ShapeDtypeStruct((rows, width), BF16),
            jax.ShapeDtypeStruct(blocks, BF16),
        ),
        in_specs=[hbm] * 5,
        out_specs=(hbm, hbm),
        scratch_shapes=[
            pltpu.VMEM((rows, width), BF16),
            pltpu.VMEM(blocks, BF16),
            pltpu.VMEM((rows, width), BF16),
            pltpu.VMEM((1, width), F32),
            pltpu.VMEM((1, width), F32),
            pltpu.VMEM((parts, width, CHUNK), BF16),
            pltpu.VMEM((width, width), BF16),
            pltpu.VMEM((rows, width), BF16),
            pltpu.VMEM((parts, rows, CHUNK), BF16),
            pltpu.VMEM((tokens, width), BF16),
            pltpu.SemaphoreType.DMA((2,)),
            pltpu.SemaphoreType.DMA((count,)),
            pltpu.SemaphoreType.DMA((parts,)),
            pltpu.SemaphoreType.DMA,
            pltpu.SemaphoreType.DMA((count,)),
            pltpu.SemaphoreType.DMA((count,)),
        ],
        compiler_params=pltpu.CompilerParams(vmem_limit_bytes=VMEM),
        cost_estimate=pl.CostEstimate(flops=16 * 10**9, bytes_accessed=14 * 2**20, transcendentals=0),
        name="spatial",
    )(frames.reshape(rows, width), gain_s.reshape(1, width), gain_t.reshape(1, width), w_qkv, w_o)


def temporal_kernel(
    local_pos,
    len_ref,
    recv_hbm,
    *refs,
):
    parts_hbm, (send_hbm, *scratch) = refs[:-13], refs[-13:]
    recv_ref, send_ref, whole, low, w_qkv, hidden, qkv, heads, cap, recv_sem, part_sem, send_sem = scratch
    count = len(parts_hbm) // 2
    parts_in = []
    for side in range(2):
        parts_in += [whole.at[3 * side + k] for k in range(3)] + [low.at[2 * side + k] for k in range(count - 3)]
    fetch_recv = pltpu.make_async_copy(recv_hbm, recv_ref, recv_sem)
    fetch_recv.start()
    fetches = [
        pltpu.make_async_copy(source, part, part_sem.at[k]) for k, (source, part) in enumerate(zip(parts_hbm, parts_in))
    ]
    total = hidden.shape[0] // local_pos
    width = hidden.shape[1]
    parts = 3 * width // CHUNK
    scale = (width // HEADS) ** (-0.5)
    groups = width // LANES
    block = local_pos * groups
    span, seen = cap.shape[1:]
    back = total - seen

    number = lax.broadcasted_iota(jnp.int32, (1, LANES), 1)

    def add(e, ends):
        return ends + jnp.where(number >= e, len_ref[e], 0)

    ends = lax.fori_loop(0, len_ref.shape[0], add, jnp.zeros((1, LANES), jnp.int32))
    position = lax.broadcasted_iota(jnp.int32, (total, LANES), 0)
    begin = jnp.max(jnp.where(ends <= position, ends, 0), axis=1, keepdims=True)
    lane = lax.broadcasted_iota(jnp.int32, (span, LANES), 1)
    for b in range(total // span):
        rows = slice(b * span, (b + 1) * span)
        for side in range(seen // LANES):
            other = lane + b * back + side * LANES
            fine = (other <= position[rows]) & (other >= begin[rows])
            cap[b, :, side * LANES : (side + 1) * LANES] = jnp.where(fine, jnp.inf, -1e30)

    step = 4 * groups
    fetch_recv.wait()
    for fetch in fetches[:count]:
        fetch.start()
    for k in range(total // step):
        wide = recv_ref[pl.ds(k * step * block, step * block), :].astype(F32)
        wide = wide.reshape(step, local_pos, groups, LANES)
        for i in range(local_pos):
            at = i * total + k * step
            hidden[at : at + step, :] = wide[:, i].reshape(step, width).astype(BF16)

    core = lax.rem(lax.axis_index("grp"), 2)
    half = parts // 2
    lines = whole.shape[1]
    for turn in range(2):
        side = core if turn == 0 else 1 - core
        for fetch in fetches[turn * count : (turn + 1) * count]:
            fetch.wait()
        if turn == 0:
            for fetch in fetches[count:]:
                fetch.start()
        put_rows(parts_in[turn * count : (turn + 1) * count], side, (0, 1, 3, 2, 2), (0, 0, 0, 0, lines // 2), w_qkv)

        @pl.loop(0, half, step=TOGETHER)
        def _(first, side=side):
            for k in range(TOGETHER):
                c = side * half + first + k
                qkv[c] = jnp.dot(hidden[...], w_qkv[c], preferred_element_type=F32).astype(BF16)

    third = parts // 3
    per = CHUNK // LANES

    @pl.loop(0, local_pos)
    def _(i):
        @pl.loop(0, total // span)
        def _(b):
            at = pl.ds(pl.multiple_of(i * total + b * span, LANES // 2), span)
            near = pl.ds(pl.multiple_of(i * total + b * back, LANES), seen)
            limit = cap[b]
            for pair in range(HEADS // 2):
                c, cols = pair // per, pl.ds((pair % per) * LANES, LANES)
                heads[at, pl.ds(pair * LANES, LANES)] = head_pair(
                    qkv[c, at, cols], qkv[third + c, near, cols], qkv[2 * third + c, near, cols], scale, limit
                )

    gives = []
    for k in range(total // step):
        both = [
            heads[i * total + k * step : i * total + (k + 1) * step, :].astype(F32).reshape(step, groups, LANES)
            for i in range(local_pos)
        ]
        wide = jnp.stack(both, axis=1).reshape(step * block, LANES)
        at = pl.ds(k * step * block, step * block)
        send_ref[at, :] = wide.astype(BF16)
        gives.append(pltpu.make_async_copy(send_ref.at[at, :], send_hbm.at[at, :], send_sem.at[k]))
        gives[k].start()
    for give in gives:
        give.wait()


def temporal(episode_len, recv, weights, total, local_pos):
    lines, rows, cols = weights[0].shape
    width = lines * SIDE * rows
    tokens = total * local_pos
    parts = 3 * width // CHUNK
    span, seen = total // 2, 2 * LANES
    hbm = pl.BlockSpec(memory_space=pl.ANY)
    return pl.pallas_call(
        functools.partial(temporal_kernel, local_pos),
        out_shape=jax.ShapeDtypeStruct(recv.shape, BF16),
        in_specs=[pl.BlockSpec(memory_space=pltpu.SMEM)] + [hbm] * (1 + len(weights)),
        out_specs=hbm,
        scratch_shapes=[
            pltpu.VMEM(recv.shape, BF16),
            pltpu.VMEM(recv.shape, BF16),
            pltpu.VMEM((6, lines, rows, cols), BF16),
            pltpu.VMEM((4, lines // 2, rows, cols), BF16),
            pltpu.VMEM((parts, width, CHUNK), BF16),
            pltpu.VMEM((tokens, width), BF16),
            pltpu.VMEM((parts, tokens, CHUNK), BF16),
            pltpu.VMEM((tokens, width), BF16),
            pltpu.VMEM((total // span, span, seen), F32),
            pltpu.SemaphoreType.DMA,
            pltpu.SemaphoreType.DMA((len(weights),)),
            pltpu.SemaphoreType.DMA((total // 32,)),
        ],
        compiler_params=pltpu.CompilerParams(vmem_limit_bytes=VMEM),
        cost_estimate=pl.CostEstimate(flops=16 * 10**9, bytes_accessed=14 * 2**20, transcendentals=0),
        name="temporal",
    )(episode_len, recv, *weights)


def finish_kernel(tokens, mixed_hbm, recv_hbm, *refs):
    parts_hbm, (out_hbm, *scratch) = refs[:-11], refs[-11:]
    mixed_ref, recv_ref, out_ref, parts_in, w_o, heads, mixed_sem, recv_sem, part_sem, out_sem = scratch
    rows, width = mixed_ref.shape
    count = rows // tokens
    groups = width // LANES
    owners = tokens // 2

    def slab(f):
        return pl.ds(f * 2 * groups, 2 * groups)

    def frame(f):
        return pl.ds(f * tokens, tokens)

    got = [
        pltpu.make_async_copy(recv_hbm.at[:, slab(f), :], recv_ref.at[:, slab(f), :], recv_sem.at[f])
        for f in range(count)
    ]
    had = [
        pltpu.make_async_copy(mixed_hbm.at[frame(f), :], mixed_ref.at[frame(f), :], mixed_sem.at[f])
        for f in range(count)
    ]
    fetches = [
        pltpu.make_async_copy(source, parts_in.at[k], part_sem.at[k]) for k, source in enumerate(parts_hbm)
    ]
    gives = [
        pltpu.make_async_copy(out_ref.at[frame(f), :], out_hbm.at[frame(f), :], out_sem.at[f]) for f in range(count)
    ]
    for copy in got[:1] + fetches + had[:1] + got[1:] + had[1:]:
        copy.start()
    for f in range(count):
        got[f].wait()
        wide = recv_ref[:, slab(f), :].astype(F32)
        wide = wide.reshape(owners, 2, groups, LANES)
        for i in range(2):
            heads[i * owners : (i + 1) * owners, :] = wide[:, i].reshape(owners, width).astype(BF16)
        if f == 0:
            for copy in fetches:
                copy.wait()
            core = lax.rem(lax.axis_index("grp"), 2)
            for turn in range(2):
                mine = [parts_in.at[turn * SIDE + k] for k in range(SIDE)]
                put_rows(mine, core if turn == 0 else 1 - core, (0, 1, 3, 2), (0, 0, 0, 0), w_o)
        had[f].wait()
        for c in range(width // CHUNK):
            cols = pl.ds(c * CHUNK, CHUNK)
            update = jnp.dot(heads[...], w_o[c], preferred_element_type=F32).astype(BF16)
            out_ref[frame(f), cols] = (mixed_ref[frame(f), cols].astype(F32) + update.astype(F32)).astype(BF16)
        gives[f].start()
    for give in gives:
        give.wait()


def finish(mixed, recv, weights, tokens):
    lines, rows, cols = weights[0].shape
    width = mixed.shape[1]
    count = mixed.shape[0] // tokens
    hbm = pl.BlockSpec(memory_space=pl.ANY)
    return pl.pallas_call(
        functools.partial(finish_kernel, tokens),
        out_shape=jax.ShapeDtypeStruct(mixed.shape, BF16),
        in_specs=[hbm] * (2 + len(weights)),
        out_specs=hbm,
        scratch_shapes=[
            pltpu.VMEM(mixed.shape, BF16),
            pltpu.VMEM(recv.shape, BF16),
            pltpu.VMEM(mixed.shape, BF16),
            pltpu.VMEM((len(weights), lines, rows, cols), BF16),
            pltpu.VMEM((2 * cols // CHUNK, width, CHUNK), BF16),
            pltpu.VMEM((tokens, width), BF16),
            pltpu.SemaphoreType.DMA((count,)),
            pltpu.SemaphoreType.DMA((count,)),
            pltpu.SemaphoreType.DMA((len(weights),)),
            pltpu.SemaphoreType.DMA((count,)),
        ],
        compiler_params=pltpu.CompilerParams(vmem_limit_bytes=VMEM),
        cost_estimate=pl.CostEstimate(flops=2 * 10**9, bytes_accessed=6 * 2**20, transcendentals=0),
        name="finish",
    )(mixed, recv, *weights)


AXES = ("dp", "grp")
SIDE = 4


def device(z, y, x, core):
    return ((z * SIDE + y) * SIDE + x % SIDE) * 2 + core


def swap_halves(shard):
    span = range(SIDE)
    pairs = [[device(z, y, x, 0), device(z, y, x, 1)] for z in span for y in span for x in span]
    return lax.all_to_all(shard, AXES, split_axis=1, concat_axis=0, tiled=True, axis_index_groups=pairs)


def spread(block):
    span = range(SIDE)
    planes = [[device(z, y, x, core) for z in span for y in span] for x in span for core in range(2)]
    copies = jnp.broadcast_to(block[None], (len(planes[0]),) + block.shape)
    return lax.all_to_all(copies, AXES, split_axis=0, concat_axis=0, tiled=True, axis_index_groups=planes)


def along_x(part, step):
    span = range(SIDE)
    places = [(z, y, x, core) for z in span for y in span for x in span for core in range(2)]
    pairs = [(device(z, y, x, core), device(z, y, x + step, core)) for z, y, x, core in places]
    return lax.ppermute(part, AXES, pairs)


def from_sibling(part):
    count = lax.axis_size(AXES)
    return lax.ppermute(part, AXES, [(k, k ^ 1) for k in range(count)])


def put_rows(parts, side, shifts, lows, blocks):
    x = lax.axis_index("grp") // 2
    half = blocks.shape[0] // 2
    for part, shift, low in zip(parts, shifts, lows):
        origin = lax.rem(x + SIDE - shift, SIDE)
        lines, rows, _ = part.shape
        for line in range(lines):
            at = pl.ds(pl.multiple_of(((low + line) * SIDE + origin) * rows, rows), rows)
            for c in range(half):
                blocks[side * half + c, at, :] = part[line, :, c * CHUNK : (c + 1) * CHUNK]


def exchange(array, shards):
    blocks = array.reshape(shards, -1, LANES)
    return lax.all_to_all(blocks, AXES, split_axis=0, concat_axis=0, tiled=True)


def local(frames, episode_len, norm_spatial, w_sqkv, w_so, norm_temporal, w_tqkv, w_to):
    count, tokens, width = frames.shape
    shards = lax.axis_size(AXES)
    cut = 3 * width // 2
    halves = [w_tqkv[:, :cut], w_to[:, : width // 2], w_tqkv[:, cut:], w_to[:, width // 2 :]]
    plane = spread(swap_halves(jnp.concatenate(halves, axis=1)))
    mixed, send = spatial(frames, norm_spatial, norm_temporal, w_sqkv, w_so)
    plane, send = lax.optimization_barrier((plane, send))
    own, own_o = plane[:, :, :cut], plane[:, :, cut:]
    left, right = along_x(own, 1), along_x(own, -1)
    lines = plane.shape[0]
    low, high, left, right = lax.optimization_barrier((left[: lines // 2], right[lines // 2 :], left, right))
    mine = [own, left, right, along_x(low, 1), along_x(high, -1)]
    theirs = [from_sibling(part) for part in mine]
    recv = exchange(send, shards)
    recv, own_o = lax.optimization_barrier((recv, own_o))
    mine_o = [own_o] + [along_x(own_o, step) for step in (1, -1, 2)]
    back = temporal(episode_len, recv.reshape(-1, LANES), mine + theirs, count * shards, tokens // shards)
    back, mine_o = lax.optimization_barrier((back, mine_o))
    theirs_o = [from_sibling(part) for part in mine_o]
    returned = exchange(back, shards)
    return finish(mixed, returned, mine_o + theirs_o, tokens).reshape(frames.shape)


def solution(mesh):
    placed = (
        P(("dp", "grp"), None, None),
        P(),
        P(),
        P(),
        P(),
        P(),
        P(("dp", "grp"), None),
        P(("dp", "grp"), None),
    )
    return jax.shard_map(
        local, mesh=mesh, in_specs=placed, out_specs=P(("dp", "grp"), None, None), check_vma=False
    )
```

```python
import functools

import jax
import jax.numpy as jnp
from jax import lax
from jax.experimental import pallas as pl
from jax.experimental.pallas import tpu as pltpu
from jax.sharding import PartitionSpec as P

HEADS = 16
LANES = 128
CHUNK = 256
TOGETHER = 3
VMEM = 63 * 10**6
LOG2E = 1.4426950408889634
F32 = jnp.float32
BF16 = jnp.bfloat16


def normed(wide, gain):
    scale = lax.rsqrt(jnp.mean(wide * wide, axis=-1, keepdims=True) + 1e-06)
    return wide * scale * gain


def head_pair(q2, k2, v2, scale, cap=None):
    lane = lax.broadcasted_iota(jnp.int32, q2.shape, 1)
    zero = jnp.zeros_like(q2)
    outs = []
    for side in range(2):
        mine = lane < 64 if side == 0 else lane >= 64
        q = jnp.where(mine, q2, zero)
        scores = lax.dot_general(q, k2, (((1,), (1,)), ((), ())), preferred_element_type=F32)
        if cap is not None:
            scores = jnp.minimum(scores, cap)
        top = jnp.max(scores, axis=-1, keepdims=True)
        weights = jnp.exp2((scores - top) * (scale * LOG2E))
        both = jnp.concatenate([v2, jnp.ones_like(v2)], axis=1)
        out = jnp.dot(weights.astype(BF16), both, preferred_element_type=F32)
        outs.append(out[:, :LANES] / out[:, LANES:])
    return jnp.where(lane < 64, outs[0], outs[1]).astype(BF16)


def spatial_kernel(
    tokens,
    frames_hbm,
    gain_s_hbm,
    gain_t_hbm,
    w_qkv_hbm,
    w_o_hbm,
    mixed_hbm,
    send_hbm,
    mixed_ref,
    send_ref,
    frames_ref,
    gain_s_ref,
    gain_t_ref,
    w_qkv,
    w_o,
    hidden,
    qkv,
    heads,
    gain_sem,
    frame_sem,
    qkv_sem,
    o_sem,
    mixed_sem,
    send_sem,
):
    rows, width = frames_ref.shape
    count = rows // tokens
    parts = 3 * width // CHUNK
    scale = (width // HEADS) ** (-0.5)
    groups = width // LANES
    owners = tokens // 2

    def fetch(c):
        return pltpu.make_async_copy(
            w_qkv_hbm.at[:, pl.ds(pl.multiple_of(c * CHUNK, CHUNK), CHUNK)], w_qkv.at[c], qkv_sem.at[c]
        )

    fetch_o = pltpu.make_async_copy(w_o_hbm, w_o, o_sem)

    def fetch_frame(f):
        at = pl.ds(pl.multiple_of(f * tokens, tokens), tokens)
        return pltpu.make_async_copy(frames_hbm.at[at, :], frames_ref.at[at, :], frame_sem.at[f])

    def give_mixed(f):
        at = pl.ds(pl.multiple_of(f * tokens, tokens), tokens)
        return pltpu.make_async_copy(mixed_ref.at[at, :], mixed_hbm.at[at, :], mixed_sem.at[f])

    def give_send(f):
        at = pl.ds(pl.multiple_of(f * 2 * groups, 2 * groups), 2 * groups)
        return pltpu.make_async_copy(send_ref.at[:, at, :], send_hbm.at[:, at, :], send_sem.at[f])

    gains = (
        pltpu.make_async_copy(gain_s_hbm, gain_s_ref, gain_sem.at[0]),
        pltpu.make_async_copy(gain_t_hbm, gain_t_ref, gain_sem.at[1]),
    )
    for copy in gains:
        copy.start()
    for f in range(count):
        fetch_frame(f).start()
    for copy in gains:
        copy.wait()

    @pl.loop(0, count)
    def _(f):
        at = pl.ds(pl.multiple_of(f * tokens, tokens), tokens)
        fetch_frame(f).wait()
        for c in range(parts // 4):
            fetch(f * (parts // 4) + c).start()
        hidden[at, :] = normed(frames_ref[at, :].astype(F32), gain_s_ref[...]).astype(BF16)

    for c in range(count * (parts // 4), parts):
        fetch(c).start()
    fetch_o.start()

    @pl.loop(0, parts, step=TOGETHER)
    def _(first):
        for c in range(TOGETHER):
            fetch(first + c).wait()
        for c in range(TOGETHER):
            qkv[first + c] = jnp.dot(hidden[...], w_qkv[first + c], preferred_element_type=F32).astype(BF16)

    fetch_o.wait()
    third = parts // 3
    per = CHUNK // LANES

    for f in range(count):
        at = pl.ds(f * tokens, tokens)
        for pair in range(HEADS // 2):
            c, cols = pair // per, pl.ds((pair % per) * LANES, LANES)
            heads[:, pair * LANES : (pair + 1) * LANES] = head_pair(
                qkv[c, at, cols], qkv[third + c, at, cols], qkv[2 * third + c, at, cols], scale
            )
        update = jnp.dot(heads[...], w_o[...], preferred_element_type=F32)
        mixed = (frames_ref[at, :].astype(F32) + update).astype(BF16)
        mixed_ref[at, :] = mixed
        inner = normed(mixed.astype(F32), gain_t_ref[...])
        both = [inner[i * owners : (i + 1) * owners].reshape(owners, groups, LANES) for i in range(2)]
        rows_out = pl.ds(pl.multiple_of(f * 2 * groups, 2 * groups), 2 * groups)
        send_ref[:, rows_out, :] = jnp.concatenate(both, axis=1).astype(BF16)
        give_mixed(f).start()
        give_send(f).start()

    for f in range(count):
        give_mixed(f).wait()
        give_send(f).wait()


def spatial(frames, gain_s, gain_t, w_qkv, w_o):
    count, tokens, width = frames.shape
    rows = count * tokens
    parts = 3 * width // CHUNK
    blocks = (tokens // 2, count * 2 * width // LANES, LANES)
    hbm = pl.BlockSpec(memory_space=pl.ANY)
    return pl.pallas_call(
        functools.partial(spatial_kernel, tokens),
        out_shape=(
            jax.ShapeDtypeStruct((rows, width), BF16),
            jax.ShapeDtypeStruct(blocks, BF16),
        ),
        in_specs=[hbm] * 5,
        out_specs=(hbm, hbm),
        scratch_shapes=[
            pltpu.VMEM((rows, width), BF16),
            pltpu.VMEM(blocks, BF16),
            pltpu.VMEM((rows, width), BF16),
            pltpu.VMEM((1, width), F32),
            pltpu.VMEM((1, width), F32),
            pltpu.VMEM((parts, width, CHUNK), BF16),
            pltpu.VMEM((width, width), BF16),
            pltpu.VMEM((rows, width), BF16),
            pltpu.VMEM((parts, rows, CHUNK), BF16),
            pltpu.VMEM((tokens, width), BF16),
            pltpu.SemaphoreType.DMA((2,)),
            pltpu.SemaphoreType.DMA((count,)),
            pltpu.SemaphoreType.DMA((parts,)),
            pltpu.SemaphoreType.DMA,
            pltpu.SemaphoreType.DMA((count,)),
            pltpu.SemaphoreType.DMA((count,)),
        ],
        compiler_params=pltpu.CompilerParams(vmem_limit_bytes=VMEM),
        cost_estimate=pl.CostEstimate(flops=16 * 10**9, bytes_accessed=14 * 2**20, transcendentals=0),
        name="spatial",
    )(frames.reshape(rows, width), gain_s.reshape(1, width), gain_t.reshape(1, width), w_qkv, w_o)


def temporal_kernel(
    local_pos,
    len_ref,
    recv_hbm,
    *refs,
):
    parts_hbm, (send_hbm, *scratch) = refs[:-13], refs[-13:]
    recv_ref, send_ref, whole, low, w_qkv, hidden, qkv, heads, cap, recv_sem, part_sem, send_sem = scratch
    count = len(parts_hbm) // 2
    parts_in = []
    for side in range(2):
        parts_in += [whole.at[3 * side + k] for k in range(3)] + [low.at[2 * side + k] for k in range(count - 3)]
    fetch_recv = pltpu.make_async_copy(recv_hbm, recv_ref, recv_sem)
    fetch_recv.start()
    fetches = [
        pltpu.make_async_copy(source, part, part_sem.at[k]) for k, (source, part) in enumerate(zip(parts_hbm, parts_in))
    ]
    total = hidden.shape[0] // local_pos
    width = hidden.shape[1]
    parts = 3 * width // CHUNK
    scale = (width // HEADS) ** (-0.5)
    groups = width // LANES
    block = local_pos * groups
    span, seen = cap.shape[1:]
    back = total - seen

    number = lax.broadcasted_iota(jnp.int32, (1, LANES), 1)

    def add(e, ends):
        return ends + jnp.where(number >= e, len_ref[e], 0)

    ends = lax.fori_loop(0, len_ref.shape[0], add, jnp.zeros((1, LANES), jnp.int32))
    position = lax.broadcasted_iota(jnp.int32, (total, LANES), 0)
    begin = jnp.max(jnp.where(ends <= position, ends, 0), axis=1, keepdims=True)
    lane = lax.broadcasted_iota(jnp.int32, (span, LANES), 1)
    for b in range(total // span):
        rows = slice(b * span, (b + 1) * span)
        for side in range(seen // LANES):
            other = lane + b * back + side * LANES
            fine = (other <= position[rows]) & (other >= begin[rows])
            cap[b, :, side * LANES : (side + 1) * LANES] = jnp.where(fine, jnp.inf, -1e30)

    step = 4 * groups
    fetch_recv.wait()
    for fetch in fetches[:count]:
        fetch.start()
    for k in range(total // step):
        wide = recv_ref[pl.ds(k * step * block, step * block), :].astype(F32)
        wide = wide.reshape(step, local_pos, groups, LANES)
        for i in range(local_pos):
            at = i * total + k * step
            hidden[at : at + step, :] = wide[:, i].reshape(step, width).astype(BF16)

    core = lax.rem(lax.axis_index("grp"), 2)
    half = parts // 2
    lines = whole.shape[1]
    for turn in range(2):
        side = core if turn == 0 else 1 - core
        for fetch in fetches[turn * count : (turn + 1) * count]:
            fetch.wait()
        if turn == 0:
            for fetch in fetches[count:]:
                fetch.start()
        put_rows(parts_in[turn * count : (turn + 1) * count], side, (0, 1, 3, 2, 2), (0, 0, 0, 0, lines // 2), w_qkv)

        @pl.loop(0, half, step=TOGETHER)
        def _(first, side=side):
            for k in range(TOGETHER):
                c = side * half + first + k
                qkv[c] = jnp.dot(hidden[...], w_qkv[c], preferred_element_type=F32).astype(BF16)

    third = parts // 3
    per = CHUNK // LANES

    @pl.loop(0, local_pos)
    def _(i):
        for b in range(total // span):
            at = pl.ds(pl.multiple_of(i * total + b * span, LANES // 2), span)
            near = pl.ds(pl.multiple_of(i * total + b * back, LANES), seen)
            limit = cap[b]
            for pair in range(HEADS // 2):
                c, cols = pair // per, pl.ds((pair % per) * LANES, LANES)
                heads[at, pl.ds(pair * LANES, LANES)] = head_pair(
                    qkv[c, at, cols], qkv[third + c, near, cols], qkv[2 * third + c, near, cols], scale, limit
                )

    gives = []
    for k in range(total // step):
        both = [
            heads[i * total + k * step : i * total + (k + 1) * step, :].astype(F32).reshape(step, groups, LANES)
            for i in range(local_pos)
        ]
        wide = jnp.stack(both, axis=1).reshape(step * block, LANES)
        at = pl.ds(k * step * block, step * block)
        send_ref[at, :] = wide.astype(BF16)
        gives.append(pltpu.make_async_copy(send_ref.at[at, :], send_hbm.at[at, :], send_sem.at[k]))
        gives[k].start()
    for give in gives:
        give.wait()


def temporal(episode_len, recv, weights, total, local_pos):
    lines, rows, cols = weights[0].shape
    width = lines * SIDE * rows
    tokens = total * local_pos
    parts = 3 * width // CHUNK
    span, seen = total // 2, 2 * LANES
    hbm = pl.BlockSpec(memory_space=pl.ANY)
    return pl.pallas_call(
        functools.partial(temporal_kernel, local_pos),
        out_shape=jax.ShapeDtypeStruct(recv.shape, BF16),
        in_specs=[pl.BlockSpec(memory_space=pltpu.SMEM)] + [hbm] * (1 + len(weights)),
        out_specs=hbm,
        scratch_shapes=[
            pltpu.VMEM(recv.shape, BF16),
            pltpu.VMEM(recv.shape, BF16),
            pltpu.VMEM((6, lines, rows, cols), BF16),
            pltpu.VMEM((4, lines // 2, rows, cols), BF16),
            pltpu.VMEM((parts, width, CHUNK), BF16),
            pltpu.VMEM((tokens, width), BF16),
            pltpu.VMEM((parts, tokens, CHUNK), BF16),
            pltpu.VMEM((tokens, width), BF16),
            pltpu.VMEM((total // span, span, seen), F32),
            pltpu.SemaphoreType.DMA,
            pltpu.SemaphoreType.DMA((len(weights),)),
            pltpu.SemaphoreType.DMA((total // 32,)),
        ],
        compiler_params=pltpu.CompilerParams(vmem_limit_bytes=VMEM),
        cost_estimate=pl.CostEstimate(flops=16 * 10**9, bytes_accessed=14 * 2**20, transcendentals=0),
        name="temporal",
    )(episode_len, recv, *weights)


def finish_kernel(tokens, mixed_hbm, recv_hbm, *refs):
    parts_hbm, (out_hbm, *scratch) = refs[:-11], refs[-11:]
    mixed_ref, recv_ref, out_ref, parts_in, w_o, heads, mixed_sem, recv_sem, part_sem, out_sem = scratch
    rows, width = mixed_ref.shape
    count = rows // tokens
    groups = width // LANES
    owners = tokens // 2

    def slab(f):
        return pl.ds(f * 2 * groups, 2 * groups)

    def frame(f):
        return pl.ds(f * tokens, tokens)

    got = [
        pltpu.make_async_copy(recv_hbm.at[:, slab(f), :], recv_ref.at[:, slab(f), :], recv_sem.at[f])
        for f in range(count)
    ]
    had = [
        pltpu.make_async_copy(mixed_hbm.at[frame(f), :], mixed_ref.at[frame(f), :], mixed_sem.at[f])
        for f in range(count)
    ]
    fetches = [
        pltpu.make_async_copy(source, parts_in.at[k], part_sem.at[k]) for k, source in enumerate(parts_hbm)
    ]
    gives = [
        pltpu.make_async_copy(out_ref.at[frame(f), :], out_hbm.at[frame(f), :], out_sem.at[f]) for f in range(count)
    ]
    for copy in got[:1] + fetches + had[:1] + got[1:] + had[1:]:
        copy.start()
    for f in range(count):
        got[f].wait()
        wide = recv_ref[:, slab(f), :].astype(F32)
        wide = wide.reshape(owners, 2, groups, LANES)
        for i in range(2):
            heads[i * owners : (i + 1) * owners, :] = wide[:, i].reshape(owners, width).astype(BF16)
        if f == 0:
            for copy in fetches:
                copy.wait()
            core = lax.rem(lax.axis_index("grp"), 2)
            for turn in range(2):
                mine = [parts_in.at[turn * SIDE + k] for k in range(SIDE)]
                put_rows(mine, core if turn == 0 else 1 - core, (0, 1, 3, 2), (0, 0, 0, 0), w_o)
        had[f].wait()
        for c in range(width // CHUNK):
            cols = pl.ds(c * CHUNK, CHUNK)
            update = jnp.dot(heads[...], w_o[c], preferred_element_type=F32).astype(BF16)
            out_ref[frame(f), cols] = (mixed_ref[frame(f), cols].astype(F32) + update.astype(F32)).astype(BF16)
        gives[f].start()
    for give in gives:
        give.wait()


def finish(mixed, recv, weights, tokens):
    lines, rows, cols = weights[0].shape
    width = mixed.shape[1]
    count = mixed.shape[0] // tokens
    hbm = pl.BlockSpec(memory_space=pl.ANY)
    return pl.pallas_call(
        functools.partial(finish_kernel, tokens),
        out_shape=jax.ShapeDtypeStruct(mixed.shape, BF16),
        in_specs=[hbm] * (2 + len(weights)),
        out_specs=hbm,
        scratch_shapes=[
            pltpu.VMEM(mixed.shape, BF16),
            pltpu.VMEM(recv.shape, BF16),
            pltpu.VMEM(mixed.shape, BF16),
            pltpu.VMEM((len(weights), lines, rows, cols), BF16),
            pltpu.VMEM((2 * cols // CHUNK, width, CHUNK), BF16),
            pltpu.VMEM((tokens, width), BF16),
            pltpu.SemaphoreType.DMA((count,)),
            pltpu.SemaphoreType.DMA((count,)),
            pltpu.SemaphoreType.DMA((len(weights),)),
            pltpu.SemaphoreType.DMA((count,)),
        ],
        compiler_params=pltpu.CompilerParams(vmem_limit_bytes=VMEM - 2 * 2**20),
        cost_estimate=pl.CostEstimate(flops=2 * 10**9, bytes_accessed=6 * 2**20, transcendentals=0),
        name="finish",
    )(mixed, recv, *weights)


AXES = ("dp", "grp")
SIDE = 4


def device(z, y, x, core):
    return ((z * SIDE + y) * SIDE + x % SIDE) * 2 + core


def swap_halves(shard):
    span = range(SIDE)
    pairs = [[device(z, y, x, 0), device(z, y, x, 1)] for z in span for y in span for x in span]
    return lax.all_to_all(shard, AXES, split_axis=1, concat_axis=0, tiled=True, axis_index_groups=pairs)


def spread(block):
    span = range(SIDE)
    planes = [[device(z, y, x, core) for z in span for y in span] for x in span for core in range(2)]
    copies = jnp.broadcast_to(block[None], (len(planes[0]),) + block.shape)
    return lax.all_to_all(copies, AXES, split_axis=0, concat_axis=0, tiled=True, axis_index_groups=planes)


def along_x(part, step):
    span = range(SIDE)
    places = [(z, y, x, core) for z in span for y in span for x in span for core in range(2)]
    pairs = [(device(z, y, x, core), device(z, y, x + step, core)) for z, y, x, core in places]
    return lax.ppermute(part, AXES, pairs)


def from_sibling(part):
    count = lax.axis_size(AXES)
    return lax.ppermute(part, AXES, [(k, k ^ 1) for k in range(count)])


def put_rows(parts, side, shifts, lows, blocks):
    x = lax.axis_index("grp") // 2
    half = blocks.shape[0] // 2
    for part, shift, low in zip(parts, shifts, lows):
        origin = lax.rem(x + SIDE - shift, SIDE)
        lines, rows, _ = part.shape
        for line in range(lines):
            at = pl.ds(pl.multiple_of(((low + line) * SIDE + origin) * rows, rows), rows)
            for c in range(half):
                blocks[side * half + c, at, :] = part[line, :, c * CHUNK : (c + 1) * CHUNK]


def exchange(array, shards):
    blocks = array.reshape(shards, -1, LANES)
    return lax.all_to_all(blocks, AXES, split_axis=0, concat_axis=0, tiled=True)


def local(frames, episode_len, norm_spatial, w_sqkv, w_so, norm_temporal, w_tqkv, w_to):
    count, tokens, width = frames.shape
    shards = lax.axis_size(AXES)
    cut = 3 * width // 2
    halves = [w_tqkv[:, :cut], w_to[:, : width // 2], w_tqkv[:, cut:], w_to[:, width // 2 :]]
    plane = spread(swap_halves(jnp.concatenate(halves, axis=1)))
    mixed, send = spatial(frames, norm_spatial, norm_temporal, w_sqkv, w_so)
    plane, send = lax.optimization_barrier((plane, send))
    own, own_o = plane[:, :, :cut], plane[:, :, cut:]
    left, right = along_x(own, 1), along_x(own, -1)
    lines = plane.shape[0]
    low, high, left, right = lax.optimization_barrier((left[: lines // 2], right[lines // 2 :], left, right))
    mine = [own, left, right, along_x(low, 1), along_x(high, -1)]
    theirs = [from_sibling(part) for part in mine]
    recv = exchange(send, shards)
    recv, own_o = lax.optimization_barrier((recv, own_o))
    mine_o = [own_o] + [along_x(own_o, step) for step in (1, -1, 2)]
    back = temporal(episode_len, recv.reshape(-1, LANES), mine + theirs, count * shards, tokens // shards)
    back, mine_o = lax.optimization_barrier((back, mine_o))
    theirs_o = [from_sibling(part) for part in mine_o]
    returned = exchange(back, shards)
    return finish(mixed, returned, mine_o + theirs_o, tokens).reshape(frames.shape)


def solution(mesh):
    placed = (
        P(("dp", "grp"), None, None),
        P(),
        P(),
        P(),
        P(),
        P(),
        P(("dp", "grp"), None),
        P(("dp", "grp"), None),
    )
    return jax.shard_map(
        local, mesh=mesh, in_specs=placed, out_specs=P(("dp", "grp"), None, None), check_vma=False
    )
```

```python
import functools

import jax
import jax.numpy as jnp
from jax import lax
from jax.experimental import pallas as pl
from jax.experimental.pallas import tpu as pltpu
from jax.sharding import PartitionSpec as P

HEADS = 16
LANES = 128
CHUNK = 256
TOGETHER = 3
VMEM = 63 * 10**6
LOG2E = 1.4426950408889634
F32 = jnp.float32
BF16 = jnp.bfloat16


def normed(wide, gain):
    scale = lax.rsqrt(jnp.mean(wide * wide, axis=-1, keepdims=True) + 1e-06)
    return wide * scale * gain


def head_pair(q2, k2, v2, scale, cap=None):
    lane = lax.broadcasted_iota(jnp.int32, q2.shape, 1)
    zero = jnp.zeros_like(q2)
    outs = []
    for side in range(2):
        mine = lane < 64 if side == 0 else lane >= 64
        q = jnp.where(mine, q2, zero)
        scores = lax.dot_general(q, k2, (((1,), (1,)), ((), ())), preferred_element_type=F32)
        if cap is not None:
            scores = jnp.minimum(scores, cap)
        top = jnp.max(scores, axis=-1, keepdims=True)
        weights = jnp.exp2((scores - top) * (scale * LOG2E))
        both = jnp.concatenate([v2, jnp.ones_like(v2)], axis=1)
        out = jnp.dot(weights.astype(BF16), both, preferred_element_type=F32)
        outs.append(out[:, :LANES] / out[:, LANES:])
    return jnp.where(lane < 64, outs[0], outs[1]).astype(BF16)


def spatial_kernel(
    tokens,
    frames_hbm,
    gain_s_hbm,
    gain_t_hbm,
    w_qkv_hbm,
    w_o_hbm,
    mixed_hbm,
    send_hbm,
    mixed_ref,
    send_ref,
    frames_ref,
    gain_s_ref,
    gain_t_ref,
    w_qkv,
    w_o,
    hidden,
    qkv,
    heads,
    gain_sem,
    frame_sem,
    qkv_sem,
    o_sem,
    mixed_sem,
    send_sem,
):
    rows, width = frames_ref.shape
    count = rows // tokens
    parts = 3 * width // CHUNK
    scale = (width // HEADS) ** (-0.5)
    groups = width // LANES
    owners = tokens // 2

    def fetch(c):
        return pltpu.make_async_copy(
            w_qkv_hbm.at[:, pl.ds(pl.multiple_of(c * CHUNK, CHUNK), CHUNK)], w_qkv.at[c], qkv_sem.at[c]
        )

    fetch_o = pltpu.make_async_copy(w_o_hbm, w_o, o_sem)

    def fetch_frame(f):
        at = pl.ds(pl.multiple_of(f * tokens, tokens), tokens)
        return pltpu.make_async_copy(frames_hbm.at[at, :], frames_ref.at[at, :], frame_sem.at[f])

    def give_mixed(f):
        at = pl.ds(pl.multiple_of(f * tokens, tokens), tokens)
        return pltpu.make_async_copy(mixed_ref.at[at, :], mixed_hbm.at[at, :], mixed_sem.at[f])

    def give_send(f):
        at = pl.ds(pl.multiple_of(f * 2 * groups, 2 * groups), 2 * groups)
        return pltpu.make_async_copy(send_ref.at[:, at, :], send_hbm.at[:, at, :], send_sem.at[f])

    gains = (
        pltpu.make_async_copy(gain_s_hbm, gain_s_ref, gain_sem.at[0]),
        pltpu.make_async_copy(gain_t_hbm, gain_t_ref, gain_sem.at[1]),
    )
    for copy in gains:
        copy.start()
    for f in range(count):
        fetch_frame(f).start()
    for copy in gains:
        copy.wait()

    @pl.loop(0, count)
    def _(f):
        at = pl.ds(pl.multiple_of(f * tokens, tokens), tokens)
        fetch_frame(f).wait()
        for c in range(parts // 4):
            fetch(f * (parts // 4) + c).start()
        hidden[at, :] = normed(frames_ref[at, :].astype(F32), gain_s_ref[...]).astype(BF16)

    for c in range(count * (parts // 4), parts):
        fetch(c).start()
    fetch_o.start()

    @pl.loop(0, parts, step=TOGETHER)
    def _(first):
        for c in range(TOGETHER):
            fetch(first + c).wait()
        for c in range(TOGETHER):
            qkv[first + c] = jnp.dot(hidden[...], w_qkv[first + c], preferred_element_type=F32).astype(BF16)

    fetch_o.wait()
    third = parts // 3
    per = CHUNK // LANES

    for f in range(count):
        at = pl.ds(f * tokens, tokens)
        for pair in range(HEADS // 2):
            c, cols = pair // per, pl.ds((pair % per) * LANES, LANES)
            heads[:, pair * LANES : (pair + 1) * LANES] = head_pair(
                qkv[c, at, cols], qkv[third + c, at, cols], qkv[2 * third + c, at, cols], scale
            )
        update = jnp.dot(heads[...], w_o[...], preferred_element_type=F32)
        mixed = (frames_ref[at, :].astype(F32) + update).astype(BF16)
        mixed_ref[at, :] = mixed
        inner = normed(mixed.astype(F32), gain_t_ref[...])
        both = [inner[i * owners : (i + 1) * owners].reshape(owners, groups, LANES) for i in range(2)]
        rows_out = pl.ds(pl.multiple_of(f * 2 * groups, 2 * groups), 2 * groups)
        send_ref[:, rows_out, :] = jnp.concatenate(both, axis=1).astype(BF16)
        give_mixed(f).start()
        give_send(f).start()

    for f in range(count):
        give_mixed(f).wait()
        give_send(f).wait()


def spatial(frames, gain_s, gain_t, w_qkv, w_o):
    count, tokens, width = frames.shape
    rows = count * tokens
    parts = 3 * width // CHUNK
    blocks = (tokens // 2, count * 2 * width // LANES, LANES)
    hbm = pl.BlockSpec(memory_space=pl.ANY)
    return pl.pallas_call(
        functools.partial(spatial_kernel, tokens),
        out_shape=(
            jax.ShapeDtypeStruct((rows, width), BF16),
            jax.ShapeDtypeStruct(blocks, BF16),
        ),
        in_specs=[hbm] * 5,
        out_specs=(hbm, hbm),
        scratch_shapes=[
            pltpu.VMEM((rows, width), BF16),
            pltpu.VMEM(blocks, BF16),
            pltpu.VMEM((rows, width), BF16),
            pltpu.VMEM((1, width), F32),
            pltpu.VMEM((1, width), F32),
            pltpu.VMEM((parts, width, CHUNK), BF16),
            pltpu.VMEM((width, width), BF16),
            pltpu.VMEM((rows, width), BF16),
            pltpu.VMEM((parts, rows, CHUNK), BF16),
            pltpu.VMEM((tokens, width), BF16),
            pltpu.SemaphoreType.DMA((2,)),
            pltpu.SemaphoreType.DMA((count,)),
            pltpu.SemaphoreType.DMA((parts,)),
            pltpu.SemaphoreType.DMA,
            pltpu.SemaphoreType.DMA((count,)),
            pltpu.SemaphoreType.DMA((count,)),
        ],
        compiler_params=pltpu.CompilerParams(vmem_limit_bytes=VMEM),
        cost_estimate=pl.CostEstimate(flops=16 * 10**9, bytes_accessed=14 * 2**20, transcendentals=0),
        name="spatial",
    )(frames.reshape(rows, width), gain_s.reshape(1, width), gain_t.reshape(1, width), w_qkv, w_o)


def temporal_kernel(
    local_pos,
    len_ref,
    recv_hbm,
    *refs,
):
    parts_hbm, (send_hbm, *scratch) = refs[:-13], refs[-13:]
    recv_ref, send_ref, whole, low, w_qkv, hidden, qkv, heads, cap, recv_sem, part_sem, send_sem = scratch
    count = len(parts_hbm) // 2
    parts_in = []
    for side in range(2):
        parts_in += [whole.at[3 * side + k] for k in range(3)] + [low.at[2 * side + k] for k in range(count - 3)]
    fetch_recv = pltpu.make_async_copy(recv_hbm, recv_ref, recv_sem)
    fetch_recv.start()
    fetches = [
        pltpu.make_async_copy(source, part, part_sem.at[k]) for k, (source, part) in enumerate(zip(parts_hbm, parts_in))
    ]
    total = hidden.shape[0] // local_pos
    width = hidden.shape[1]
    parts = 3 * width // CHUNK
    scale = (width // HEADS) ** (-0.5)
    groups = width // LANES
    block = local_pos * groups
    span, seen = cap.shape[1:]
    back = total - seen

    number = lax.broadcasted_iota(jnp.int32, (1, LANES), 1)

    def add(e, ends):
        return ends + jnp.where(number >= e, len_ref[e], 0)

    ends = lax.fori_loop(0, len_ref.shape[0], add, jnp.zeros((1, LANES), jnp.int32))
    position = lax.broadcasted_iota(jnp.int32, (total, LANES), 0)
    begin = jnp.max(jnp.where(ends <= position, ends, 0), axis=1, keepdims=True)
    lane = lax.broadcasted_iota(jnp.int32, (span, LANES), 1)
    for b in range(total // span):
        rows = slice(b * span, (b + 1) * span)
        for side in range(seen // LANES):
            other = lane + b * back + side * LANES
            fine = (other <= position[rows]) & (other >= begin[rows])
            cap[b, :, side * LANES : (side + 1) * LANES] = jnp.where(fine, jnp.inf, -1e30)

    step = 4 * groups
    fetch_recv.wait()
    for fetch in fetches[:count]:
        fetch.start()
    for k in range(total // step):
        wide = recv_ref[pl.ds(k * step * block, step * block), :].astype(F32)
        wide = wide.reshape(step, local_pos, groups, LANES)
        for i in range(local_pos):
            at = i * total + k * step
            hidden[at : at + step, :] = wide[:, i].reshape(step, width).astype(BF16)

    core = lax.rem(lax.axis_index("grp"), 2)
    half = parts // 2
    lines = whole.shape[1]
    for turn in range(2):
        side = core if turn == 0 else 1 - core
        for fetch in fetches[turn * count : (turn + 1) * count]:
            fetch.wait()
        if turn == 0:
            for fetch in fetches[count:]:
                fetch.start()
        put_rows(parts_in[turn * count : (turn + 1) * count], side, (0, 1, 3, 2, 2), (0, 0, 0, 0, lines // 2), w_qkv)

        for k in range(half):
            c = side * half + k
            qkv[c] = jnp.dot(hidden[...], w_qkv[c], preferred_element_type=F32).astype(BF16)

    third = parts // 3
    per = CHUNK // LANES

    @pl.loop(0, local_pos)
    def _(i):
        for b in range(total // span):
            at = pl.ds(pl.multiple_of(i * total + b * span, LANES // 2), span)
            near = pl.ds(pl.multiple_of(i * total + b * back, LANES), seen)
            limit = cap[b]
            for pair in range(HEADS // 2):
                c, cols = pair // per, pl.ds((pair % per) * LANES, LANES)
                heads[at, pl.ds(pair * LANES, LANES)] = head_pair(
                    qkv[c, at, cols], qkv[third + c, near, cols], qkv[2 * third + c, near, cols], scale, limit
                )

    gives = []
    for k in range(total // step):
        both = [
            heads[i * total + k * step : i * total + (k + 1) * step, :].astype(F32).reshape(step, groups, LANES)
            for i in range(local_pos)
        ]
        wide = jnp.stack(both, axis=1).reshape(step * block, LANES)
        at = pl.ds(k * step * block, step * block)
        send_ref[at, :] = wide.astype(BF16)
        gives.append(pltpu.make_async_copy(send_ref.at[at, :], send_hbm.at[at, :], send_sem.at[k]))
        gives[k].start()
    for give in gives:
        give.wait()


def temporal(episode_len, recv, weights, total, local_pos):
    lines, rows, cols = weights[0].shape
    width = lines * SIDE * rows
    tokens = total * local_pos
    parts = 3 * width // CHUNK
    span, seen = total // 2, 2 * LANES
    hbm = pl.BlockSpec(memory_space=pl.ANY)
    return pl.pallas_call(
        functools.partial(temporal_kernel, local_pos),
        out_shape=jax.ShapeDtypeStruct(recv.shape, BF16),
        in_specs=[pl.BlockSpec(memory_space=pltpu.SMEM)] + [hbm] * (1 + len(weights)),
        out_specs=hbm,
        scratch_shapes=[
            pltpu.VMEM(recv.shape, BF16),
            pltpu.VMEM(recv.shape, BF16),
            pltpu.VMEM((6, lines, rows, cols), BF16),
            pltpu.VMEM((4, lines // 2, rows, cols), BF16),
            pltpu.VMEM((parts, width, CHUNK), BF16),
            pltpu.VMEM((tokens, width), BF16),
            pltpu.VMEM((parts, tokens, CHUNK), BF16),
            pltpu.VMEM((tokens, width), BF16),
            pltpu.VMEM((total // span, span, seen), F32),
            pltpu.SemaphoreType.DMA,
            pltpu.SemaphoreType.DMA((len(weights),)),
            pltpu.SemaphoreType.DMA((total // 32,)),
        ],
        compiler_params=pltpu.CompilerParams(vmem_limit_bytes=VMEM),
        cost_estimate=pl.CostEstimate(flops=16 * 10**9, bytes_accessed=14 * 2**20, transcendentals=0),
        name="temporal",
    )(episode_len, recv, *weights)


def finish_kernel(tokens, mixed_hbm, recv_hbm, *refs):
    parts_hbm, (out_hbm, *scratch) = refs[:-11], refs[-11:]
    mixed_ref, recv_ref, out_ref, parts_in, w_o, heads, mixed_sem, recv_sem, part_sem, out_sem = scratch
    rows, width = mixed_ref.shape
    count = rows // tokens
    groups = width // LANES
    owners = tokens // 2

    def slab(f):
        return pl.ds(f * 2 * groups, 2 * groups)

    def frame(f):
        return pl.ds(f * tokens, tokens)

    got = [
        pltpu.make_async_copy(recv_hbm.at[:, slab(f), :], recv_ref.at[:, slab(f), :], recv_sem.at[f])
        for f in range(count)
    ]
    had = [
        pltpu.make_async_copy(mixed_hbm.at[frame(f), :], mixed_ref.at[frame(f), :], mixed_sem.at[f])
        for f in range(count)
    ]
    fetches = [
        pltpu.make_async_copy(source, parts_in.at[k], part_sem.at[k]) for k, source in enumerate(parts_hbm)
    ]
    gives = [
        pltpu.make_async_copy(out_ref.at[frame(f), :], out_hbm.at[frame(f), :], out_sem.at[f]) for f in range(count)
    ]
    for copy in got[:1] + fetches + had[:1] + got[1:] + had[1:]:
        copy.start()
    for f in range(count):
        got[f].wait()
        wide = recv_ref[:, slab(f), :].astype(F32)
        wide = wide.reshape(owners, 2, groups, LANES)
        for i in range(2):
            at = f * tokens + i * owners
            heads[at : at + owners, :] = wide[:, i].reshape(owners, width).astype(BF16)
    for copy in fetches + had:
        copy.wait()
    core = lax.rem(lax.axis_index("grp"), 2)
    for turn in range(2):
        mine = [parts_in.at[turn * SIDE + k] for k in range(SIDE)]
        put_rows(mine, core if turn == 0 else 1 - core, (0, 1, 3, 2), (0, 0, 0, 0), w_o)
    for f in range(count):
        for c in range(width // CHUNK):
            cols = pl.ds(c * CHUNK, CHUNK)
            update = jnp.dot(heads[frame(f), :], w_o[c], preferred_element_type=F32).astype(BF16)
            out_ref[frame(f), cols] = (mixed_ref[frame(f), cols].astype(F32) + update.astype(F32)).astype(BF16)
        gives[f].start()
    for give in gives:
        give.wait()


def finish(mixed, recv, weights, tokens):
    lines, rows, cols = weights[0].shape
    width = mixed.shape[1]
    count = mixed.shape[0] // tokens
    hbm = pl.BlockSpec(memory_space=pl.ANY)
    return pl.pallas_call(
        functools.partial(finish_kernel, tokens),
        out_shape=jax.ShapeDtypeStruct(mixed.shape, BF16),
        in_specs=[hbm] * (2 + len(weights)),
        out_specs=hbm,
        scratch_shapes=[
            pltpu.VMEM(mixed.shape, BF16),
            pltpu.VMEM(recv.shape, BF16),
            pltpu.VMEM(mixed.shape, BF16),
            pltpu.VMEM((len(weights), lines, rows, cols), BF16),
            pltpu.VMEM((2 * cols // CHUNK, width, CHUNK), BF16),
            pltpu.VMEM(mixed.shape, BF16),
            pltpu.SemaphoreType.DMA((count,)),
            pltpu.SemaphoreType.DMA((count,)),
            pltpu.SemaphoreType.DMA((len(weights),)),
            pltpu.SemaphoreType.DMA((count,)),
        ],
        compiler_params=pltpu.CompilerParams(vmem_limit_bytes=VMEM),
        cost_estimate=pl.CostEstimate(flops=2 * 10**9, bytes_accessed=6 * 2**20, transcendentals=0),
        name="finish",
    )(mixed, recv, *weights)


AXES = ("dp", "grp")
SIDE = 4


def device(z, y, x, core):
    return ((z * SIDE + y) * SIDE + x % SIDE) * 2 + core


def swap_halves(shard):
    span = range(SIDE)
    pairs = [[device(z, y, x, 0), device(z, y, x, 1)] for z in span for y in span for x in span]
    return lax.all_to_all(shard, AXES, split_axis=1, concat_axis=0, tiled=True, axis_index_groups=pairs)


def spread(block):
    span = range(SIDE)
    planes = [[device(z, y, x, core) for z in span for y in span] for x in span for core in range(2)]
    copies = jnp.broadcast_to(block[None], (len(planes[0]),) + block.shape)
    return lax.all_to_all(copies, AXES, split_axis=0, concat_axis=0, tiled=True, axis_index_groups=planes)


def along_x(part, step):
    span = range(SIDE)
    places = [(z, y, x, core) for z in span for y in span for x in span for core in range(2)]
    pairs = [(device(z, y, x, core), device(z, y, x + step, core)) for z, y, x, core in places]
    return lax.ppermute(part, AXES, pairs)


def from_sibling(part):
    count = lax.axis_size(AXES)
    return lax.ppermute(part, AXES, [(k, k ^ 1) for k in range(count)])


def put_rows(parts, side, shifts, lows, blocks):
    x = lax.axis_index("grp") // 2
    half = blocks.shape[0] // 2
    for part, shift, low in zip(parts, shifts, lows):
        origin = lax.rem(x + SIDE - shift, SIDE)
        lines, rows, _ = part.shape
        for line in range(lines):
            at = pl.ds(pl.multiple_of(((low + line) * SIDE + origin) * rows, rows), rows)
            for c in range(half):
                blocks[side * half + c, at, :] = part[line, :, c * CHUNK : (c + 1) * CHUNK]


def exchange(array, shards):
    blocks = array.reshape(shards, -1, LANES)
    return lax.all_to_all(blocks, AXES, split_axis=0, concat_axis=0, tiled=True)


def local(frames, episode_len, norm_spatial, w_sqkv, w_so, norm_temporal, w_tqkv, w_to):
    count, tokens, width = frames.shape
    shards = lax.axis_size(AXES)
    cut = 3 * width // 2
    halves = [w_tqkv[:, :cut], w_to[:, : width // 2], w_tqkv[:, cut:], w_to[:, width // 2 :]]
    plane = spread(swap_halves(jnp.concatenate(halves, axis=1)))
    mixed, send = spatial(frames, norm_spatial, norm_temporal, w_sqkv, w_so)
    plane, send = lax.optimization_barrier((plane, send))
    own, own_o = plane[:, :, :cut], plane[:, :, cut:]
    left, right = along_x(own, 1), along_x(own, -1)
    lines = plane.shape[0]
    low, high, left, right = lax.optimization_barrier((left[: lines // 2], right[lines // 2 :], left, right))
    mine = [own, left, right, along_x(low, 1), along_x(high, -1)]
    theirs = [from_sibling(part) for part in mine]
    recv = exchange(send, shards)
    recv, own_o = lax.optimization_barrier((recv, own_o))
    mine_o = [own_o] + [along_x(own_o, step) for step in (1, -1, 2)]
    back = temporal(episode_len, recv.reshape(-1, LANES), mine + theirs, count * shards, tokens // shards)
    back, mine_o = lax.optimization_barrier((back, mine_o))
    theirs_o = [from_sibling(part) for part in mine_o]
    returned = exchange(back, shards)
    return finish(mixed, returned, mine_o + theirs_o, tokens).reshape(frames.shape)


def solution(mesh):
    placed = (
        P(("dp", "grp"), None, None),
        P(),
        P(),
        P(),
        P(),
        P(),
        P(("dp", "grp"), None),
        P(("dp", "grp"), None),
    )
    return jax.shard_map(
        local, mesh=mesh, in_specs=placed, out_specs=P(("dp", "grp"), None, None), check_vma=False
    )
```
